32 devices in a mesh: gx: 8 (over z, y), gy: 4 (over x, core).
Axes of the slice: x: 2, y: 2, z: 4, core: 2. Of those that a mesh axis runs over, the one named last changes fastest.
Arguments:
- modes: bfloat16 [128, 64, 2, 3, 128], P('gx', 'gy'), may hold values from -8 to 8
Outputs:
- convective: float32 [128, 128, 128], P('gx', 'gy')
- viscous: float32 [128, 128], P('gx', 'gy')
The draws below stay inside these ranges and needn't reach their ends.
All inputs are finite; a program needn't handle non-finite values.
Results may differ from the reference program's by a relative error of at most 0.004.
Values may be sent and summed in bfloat16 or wider, within the bound.
No kernel may reach another device: no remote copies, remote signals or barrier semaphores. Data moves between devices by JAX's collectives and lax.ppermute only.
A program may use at most 64 MiB of HBM per device.

```python
import math
import jax
import jax.numpy as jnp
from jax import lax

M = 128
CZ = 2
NX = 128
NY = 64
NTOT = 16384


def draw_modes(key, part):
    base = jax.random.fold_in(key, 11)
    key_white, key_mix = jax.random.split(base, 2)
    rows_all = NX * NY * CZ * 3
    white = jax.random.normal(key_white, (rows_all, M), jnp.float32)
    mixing = jax.random.normal(key_mix, (M, M), jnp.float32) / math.sqrt(M)
    mixed = jnp.dot(white, mixing, precision=lax.Precision.HIGHEST)
    mixed = jnp.clip(mixed, -8.0, 8.0)
    return mixed.reshape(NX, NY, CZ, 3, M).astype(jnp.bfloat16)


def setup_inputs(seed: int = 0) -> dict:
    key_of = jax.random.split(jax.random.key(seed), 2)
    return {
        "modes": draw_modes(jax.random.fold_in(key_of[1], 71), 0),
    }


def fourth(padded, axis, count):

    def cut(offset):
        return lax.slice_in_dim(padded, 2 + offset, 2 + offset + count, axis=axis)
    return (8.0 * (cut(1) - cut(-1)) - (cut(2) - cut(-2))) / 12.0

def reference(modes):
    field = modes.astype(jnp.float32)
    zero_pads = [(0, 0)] * 5
    pads_x = list(zero_pads)
    pads_x[0] = (2, 2)
    pads_y = list(zero_pads)
    pads_y[1] = (2, 2)
    pads_z = list(zero_pads)
    pads_z[2] = (2, 2)
    grad_x = fourth(jnp.pad(field, pads_x, mode='wrap'), 0, NX)
    grad_y = fourth(jnp.pad(field, pads_y, mode='wrap'), 1, NY)
    grad_z = fourth(jnp.pad(field, pads_z), 2, CZ)
    gradient = jnp.stack([grad_x, grad_y, grad_z]).astype(jnp.bfloat16)
    flat_modes = modes.reshape(NTOT, 3, M)
    flat_grad = gradient.reshape(3, NTOT, 3, M)
    stacked = gradient.reshape(-1, M)
    viscous = -lax.dot_general(stacked, stacked, (((0,), (0,)), ((), ())), preferred_element_type=jnp.float32) / NTOT
    block_pts = math.gcd(NTOT, 2048)
    count_blocks = NTOT // block_pts

    def accumulate(total, index):
        start = (index * block_pts).astype(jnp.int32)
        phi_block = lax.dynamic_slice_in_dim(flat_modes, start, block_pts, 0).astype(jnp.float32)
        grad_block = lax.dynamic_slice_in_dim(flat_grad, start, block_pts, 1).astype(jnp.float32)
        pair = jnp.einsum('pai,bpak->ikbp', phi_block, grad_block).astype(jnp.bfloat16)
        right_side = phi_block.transpose(1, 0, 2).reshape(3 * block_pts, M).astype(jnp.bfloat16)
        term = jnp.dot(pair.reshape(M * M, 3 * block_pts), right_side, preferred_element_type=jnp.float32)
        return (total + term.reshape(M, M, M), None)
    total, _ = lax.scan(accumulate, jnp.zeros((M, M, M), jnp.float32), jnp.arange(count_blocks, dtype=jnp.int32))
    convective = -total / jnp.sqrt(jnp.float32(NTOT))
    return (convective, viscous)
```

```python
import functools
import math

import jax
import jax.numpy as jnp
from jax import lax
from jax.experimental import pallas as pl
from jax.experimental.pallas import tpu as pltpu
from jax.sharding import PartitionSpec as P

BF16, F32 = jnp.bfloat16, jnp.float32
VMEM = pl.BlockSpec(memory_space=pltpu.VMEM)
SMEM = pl.BlockSpec(memory_space=pltpu.SMEM)
CHUNKS = 2
GROUP = 16
K_ROWS = 4


def swap(x, axis, mask):
    return lax.ppermute(x, axis, [(i, i ^ mask) for i in range(lax.axis_size(axis))])


def gathered(x, axis):
    pieces, mask = [x], lax.axis_size(axis) // 2
    masks = [0]
    while mask:
        pieces += [swap(piece, axis, mask) for piece in pieces]
        masks += [m ^ mask for m in masks]
        mask //= 2
    return pieces, masks


def derivatives(fetch, row, cells_z):
    mid = fetch(row)
    lanes = mid.shape[-1]

    def moved(points):
        return pltpu.roll(mid, (-points) % lanes, 1)

    def stencil(p1, m1, p2, m2):
        return (8.0 * (p1 - m1) - (p2 - m2)) * (1.0 / 12.0)

    grad_x = stencil(fetch(row + 1), fetch(row - 1), fetch(row + 2), fetch(row - 2))
    grad_y = stencil(
        moved(cells_z), moved(-cells_z), moved(2 * cells_z), moved(-2 * cells_z)
    )
    level = lax.broadcasted_iota(jnp.int32, mid.shape, 1) % cells_z
    grad_z = jnp.zeros_like(mid)
    for step, weight in ((1, 8.0 / 12.0), (-1, -8.0 / 12.0), (2, -1.0 / 12.0), (-2, 1.0 / 12.0)):
        if abs(step) < cells_z:
            inside = (level + step >= 0) & (level + step < cells_z)
            grad_z = grad_z + jnp.where(inside, moved(step) * weight, 0.0)
    return grad_x, grad_y, grad_z


def prepare_kernel(plan, masks, cells_z, repeat, idx_ref, *refs):
    copies, interior, count_sources = plan
    pieces = len(masks)
    sources = [refs[s * pieces:(s + 1) * pieces] for s in range(count_sources)]
    full_ref, turned_ref, grad_ref, visc_ref = refs[count_sources * pieces:]
    rows, comps, lanes, width = full_ref.shape
    part = lanes // pieces
    me = idx_ref[0]
    own = width // pieces
    for q, mask in enumerate(masks):
        slot = pl.multiple_of((me ^ mask) * part, part)
        for source, start, stop, at in copies:
            full_ref[at:at + stop - start, :, pl.ds(slot, part), :] = sources[source][q][start:stop]

    def turn(row, carry):
        for comp in range(comps):
            flat = full_ref[row, comp].astype(F32).T
            turned_ref[row, comp] = flat.reshape(width // 8, 8, lanes)
        return carry

    lax.fori_loop(0, rows, turn, 0)
    visc_ref[...] = jnp.zeros_like(visc_ref)

    def slopes(at, row):
        mine, every = [], []
        for comp in range(comps):
            def fetch_own(r):
                block = turned_ref[r, comp, pl.ds(me * (own // 8), own // 8)]
                return block.reshape(own, lanes)

            def fetch_all(r):
                return turned_ref[r, comp].reshape(width, lanes)

            for b, value in enumerate(derivatives(fetch_own, row, cells_z)):
                value = value.astype(BF16)
                mine.append(value)
                grad_ref[at, b, comp] = jnp.concatenate([value] * repeat, 0)
            every += [v.astype(BF16) for v in derivatives(fetch_all, row, cells_z)]
        visc_ref[...] += lax.dot_general(
            jnp.concatenate(every, 1), jnp.concatenate(mine, 1), (((1,), (1,)), ((), ())),
            preferred_element_type=F32,
        )

    at = 0
    for start, stop in interior:
        def one(step, carry, start=start, at=at):
            slopes(at + step, start + step)
            return carry

        lax.fori_loop(0, stop - start, one, 0)
        at += stop - start


def main_kernel(plan, own, chunk, idx_ref, full_ref, turned_ref, grad_ref, visc_ref,
                send_ref, keep_ref, *bufs):
    interior = [r for start, stop in plan[1] for r in range(start, stop)]
    _, comps, lanes, width = full_ref.shape
    halves, block_rows = send_ref.shape[:2]
    peers = 2 * halves
    i_block = width // peers
    i_part = i_block // CHUNKS
    tile = grad_ref.shape[3]
    joint = tile // own
    me = idx_ref[1]
    depth = comps * lanes
    dests = max(1, min(halves, GROUP // i_part))

    def group(low, flip):
        def source(i):
            dest = me ^ (flip + 2 * (low + i // i_part))
            row = dest * i_block + chunk * i_part
            if i_part % 8 == 0:
                return row // 8 + (i % i_part) // 8, (i % i_part) % 8
            return row // 8, (chunk * i_part) % 8 + i % i_part

        total = None
        for first in range(0, len(interior), K_ROWS):
            buf = bufs[(first // K_ROWS) % len(bufs)]
            count = min(K_ROWS, len(interior) - first)
            for x in range(first, first + count):
                for lane in range(0, lanes, 128):
                    cut = slice(lane, lane + 128)
                    grads = [[grad_ref[x, b, a, :, cut] for a in range(comps)] for b in range(comps)]
                    for i in range(0, dests * i_part, joint):
                        phis = []
                        for a in range(comps):
                            parts = []
                            for j in range(joint):
                                lead, sub = source(i + j)
                                line = turned_ref[interior[x], a, lead, sub:sub + 1, cut]
                                parts.append(jnp.broadcast_to(line, (own if joint > 1 else 16, 128)))
                            wide = jnp.concatenate(parts, 0).astype(BF16) if joint > 1 else parts[0].astype(BF16)
                            phis.append(jnp.concatenate([wide] * (tile // wide.shape[0]), 0))
                        for b in range(comps):
                            pair = phis[0] * grads[b][0]
                            for a in range(1, comps):
                                pair = pair + phis[a] * grads[b][a]
                            column = (x - first) * depth + b * lanes + lane
                            buf[i * own:i * own + tile, column:column + 128] = pair
            right = full_ref[interior[first]:interior[first] + count].reshape(count * depth, width)
            term = jnp.dot(buf[:, :count * depth], right, preferred_element_type=F32)
            total = term if total is None else total + term
        return total.reshape(dests, i_part * own, width)

    def send_step(step, carry):
        low = step * dests
        send_ref[pl.ds(low, dests), :i_part * own] = group(low, 1).astype(BF16)
        return carry

    def keep_step(step, carry):
        low = step * dests
        keep_ref[pl.ds(low, dests), :i_part * own] = group(low, 0)
        return carry

    lax.fori_loop(0, halves // dests, send_step, 0)
    lax.fori_loop(0, halves // dests, keep_step, 0)
    if block_rows > i_part * own:
        for low in range(halves):
            for flip, ref in ((1, send_ref), (0, keep_ref)):
                dest = me ^ (flip + 2 * low)
                rows = visc_ref[pl.ds(pl.multiple_of(dest * i_block, i_block), i_block), :]
                rows = jnp.concatenate([rows, jnp.zeros((i_block, width - own), F32)], 1)
                fill = block_rows - i_part * own - i_block
                if fill:
                    rows = jnp.concatenate([rows, jnp.zeros((fill, width), F32)], 0)
                ref[low, i_part * own:] = rows.astype(ref.dtype)


def prepare(plan, masks, cells_z, idx, sources, own):
    copies, interior, _ = plan
    rows = max(at + stop - start for _, start, stop, at in copies)
    count = sum(stop - start for start, stop in interior)
    _, comps, part, width = sources[0].shape
    lanes = part * len(masks)
    tile = max(own, 16)
    return pl.pallas_call(
        functools.partial(prepare_kernel, plan, masks, cells_z, tile // own),
        out_shape=(
            jax.ShapeDtypeStruct((rows, comps, lanes, width), BF16),
            jax.ShapeDtypeStruct((rows, comps, width // 8, 8, lanes), F32),
            jax.ShapeDtypeStruct((count, comps, comps, tile, lanes), BF16),
            jax.ShapeDtypeStruct((width, own), F32),
        ),
        in_specs=[SMEM] + [VMEM] * len(sources),
        out_specs=(VMEM,) * 4,
        compiler_params=pltpu.CompilerParams(vmem_limit_bytes=48 * 2**20),
        name="prepare",
    )(idx, *sources)


def project(plan, chunk, idx, state, own, peers):
    full, turned, grad, visc = state
    _, comps, lanes, width = full.shape
    halves, i_block = peers // 2, width // peers
    i_part = i_block // CHUNKS
    rows = i_part * own + (max(16, i_block) if chunk == CHUNKS - 1 else 0)
    dests = max(1, min(halves, GROUP // i_part))
    buf = pltpu.VMEM((dests * i_part * own, K_ROWS * comps * lanes), BF16)
    flops = 2 * halves * 2 * i_part * own * grad.shape[0] * comps * lanes * width
    return pl.pallas_call(
        functools.partial(main_kernel, plan, own, chunk),
        out_shape=(
            jax.ShapeDtypeStruct((halves, rows, width), BF16),
            jax.ShapeDtypeStruct((halves, rows, width), F32),
        ),
        in_specs=[SMEM] + [VMEM] * 4,
        out_specs=(VMEM,) * 2,
        scratch_shapes=[buf] * 2,
        compiler_params=pltpu.CompilerParams(vmem_limit_bytes=48 * 2**20),
        cost_estimate=pl.CostEstimate(flops=4 * flops, bytes_accessed=4 * 2**20, transcendentals=0),
        name="project",
    )(idx, full, turned, grad, visc)


def body(modes):
    cells_x, cells_y, cells_z, comps, width = modes.shape
    peers_x, peers_y = lax.axis_size("gx"), lax.axis_size("gy")
    total_points = cells_x * cells_y * cells_z * peers_x * peers_y
    own = width // peers_y
    i_block = width // peers_x
    i_part = i_block // CHUNKS
    idx = jnp.stack([lax.axis_index("gy"), lax.axis_index("gx")]).astype(jnp.int32)
    block = modes.transpose(0, 3, 1, 2, 4).reshape(cells_x, comps, cells_y * cells_z, width)
    up = [(i, (i + 1) % peers_x) for i in range(peers_x)]
    down = [(j, i) for i, j in up]
    before = lax.ppermute(block[-2:], "gx", up)
    after = lax.ppermute(block[:2], "gx", down)
    padded = jnp.concatenate([before, block, after], 0)
    pieces, masks = gathered(padded, "gy")
    plan = (((0, 0, cells_x + 4, 0),), ((2, cells_x + 2),), 1)
    state = prepare(plan, masks, cells_z, idx, pieces, own)
    finals = []
    for chunk in range(CHUNKS):
        send, keep = project(plan, chunk, idx, state, own, peers_x)
        got = swap(send, "gx", 1)
        sums = keep + got.astype(F32)
        final = sums[0]
        for q in range(1, peers_x // 2):
            final = final + swap(sums[q].astype(BF16), "gx", 2 * q).astype(F32)
        finals.append(final)
    convective = jnp.concatenate(
        [f[:i_part * own].reshape(i_part, own, width) for f in finals], 0
    ) * (-1.0 / math.sqrt(total_points))
    viscous = finals[-1][i_part * own:i_part * own + i_block, :own] * (-1.0 / total_points)
    return (convective, viscous)


def solution(mesh):
    in_specs = (P("gx", "gy", None, None, None),)
    out_specs = (P("gx", "gy", None), P("gx", "gy"))
    return jax.shard_map(body, mesh=mesh, in_specs=in_specs, out_specs=out_specs, check_vma=False)
```

```python
import functools
import math

import jax
import jax.numpy as jnp
from jax import lax
from jax.experimental import pallas as pl
from jax.experimental.pallas import tpu as pltpu
from jax.sharding import PartitionSpec as P

BF16, F32 = jnp.bfloat16, jnp.float32
VMEM = pl.BlockSpec(memory_space=pltpu.VMEM)
SMEM = pl.BlockSpec(memory_space=pltpu.SMEM)
CHUNKS = 2
GROUP = 16
K_ROWS = 4


def swap(x, axis, mask):
    return lax.ppermute(x, axis, [(i, i ^ mask) for i in range(lax.axis_size(axis))])


def gathered(x, axis):
    pieces, mask = [x], lax.axis_size(axis) // 2
    masks = [0]
    while mask:
        pieces += [swap(piece, axis, mask) for piece in pieces]
        masks += [m ^ mask for m in masks]
        mask //= 2
    return pieces, masks


def y_and_z_weights(lanes, cells_z):
    q = lax.broadcasted_iota(jnp.int32, (lanes, lanes), 0)
    p = lax.broadcasted_iota(jnp.int32, (lanes, lanes), 1)
    apart = q - p
    around = jnp.where(apart < 0, apart + lanes, apart)
    same = lax.div(q, cells_z) == lax.div(p, cells_z)
    weights_y = jnp.zeros((lanes, lanes), F32)
    weights_z = jnp.zeros((lanes, lanes), F32)
    for step, weight in ((1, 8.0), (-1, -8.0), (2, -1.0), (-2, 1.0)):
        weights_y = weights_y + jnp.where(around == (step * cells_z) % lanes, weight, 0.0)
        weights_z = weights_z + jnp.where(same & (apart == step), weight, 0.0)
    return jnp.concatenate([weights_y, weights_z], 1).astype(BF16)


def prepare_kernel(plan, masks, cells_z, repeat, idx_ref, *refs):
    copies, interior, count_sources = plan
    pieces = len(masks)
    sources = [refs[s * pieces:(s + 1) * pieces] for s in range(count_sources)]
    full_ref, turned_ref, first_ref, grad_ref, visc_ref, slope_ref, every_ref, mine_ref = refs[count_sources * pieces:]
    rows, comps, lanes, width = full_ref.shape
    part = lanes // pieces
    me = idx_ref[0]
    own = width // pieces
    for q, mask in enumerate(masks):
        slot = pl.multiple_of((me ^ mask) * part, part)
        for source, start, stop, at in copies:
            full_ref[at:at + stop - start, :, pl.ds(slot, part), :] = sources[source][q][start:stop]

    def turn(row, carry):
        for comp in range(comps):
            flat = full_ref[row, comp].astype(F32).T
            turned_ref[row, comp] = flat.reshape(width // 8, 8, lanes)
        return carry

    lax.fori_loop(0, rows, turn, 0, unroll=4)
    weights = y_and_z_weights(lanes, cells_z)

    def slopes(at, slot, row):
        mine, every = [], []
        for comp in range(comps):
            def line(step):
                return turned_ref[row + step, comp].reshape(width, lanes)

            along_x = (8.0 * (line(1) - line(-1)) - (line(2) - line(-2))) * (1.0 / 12.0)
            others = jnp.dot(line(0).astype(BF16), weights, preferred_element_type=F32) * (1.0 / 12.0)
            for b, value in enumerate((along_x, others[:, :lanes], others[:, lanes:])):
                slope_ref[b, comp] = value.reshape(width // 8, 8, lanes)
                every.append(value.astype(BF16))
        for b in range(comps):
            for comp in range(comps):
                block = slope_ref[b, comp, pl.ds(me * (own // 8), own // 8)].reshape(own, lanes).astype(BF16)
                mine.append((b, comp, block))
                tiled = jnp.concatenate([block] * repeat, 0)
                if b == 0:
                    first_ref[at, comp] = tiled.astype(F32)
                else:
                    grad_ref[at, b - 1, comp] = tiled
        mine = [m[2] for m in sorted(mine, key=lambda m: (m[1], m[0]))]
        column = pl.ds(pl.multiple_of(slot * (comps * comps * lanes), lanes), comps * comps * lanes)
        every_ref[:, column] = jnp.concatenate(every, 1)
        mine_ref[:, column] = jnp.concatenate(mine, 1)

    batch = mine_ref.shape[1] // (comps * comps * lanes)
    steps = [(row, min(row + batch, stop)) for start, stop in interior for row in range(start, stop, batch)]
    at = 0
    for start, stop in steps:
        def one(step, carry, start=start, at=at):
            slopes(at + step, step, start + step)
            return carry

        lax.fori_loop(0, stop - start, one, 0, unroll=4)
        used = (stop - start) * comps * comps * lanes
        term = lax.dot_general(
            every_ref[:, :used], mine_ref[:, :used], (((1,), (1,)), ((), ())), preferred_element_type=F32
        )
        visc_ref[...] = term if at == 0 else visc_ref[...] + term
        at += stop - start


def main_kernel(plan, own, chunk, idx_ref, full_ref, turned_ref, first_ref, grad_ref, visc_ref,
                send_ref, keep_ref):
    interior = [r for start, stop in plan[1] for r in range(start, stop)]
    _, comps, lanes, width = full_ref.shape
    halves, block_rows = send_ref.shape[:2]
    peers = 2 * halves
    i_block = width // peers
    i_part = i_block // CHUNKS
    tile = grad_ref.shape[3]
    joint = tile // own
    me = idx_ref[1]
    depth = comps * lanes
    dests = max(1, min(halves, GROUP // i_part))

    def group(low, flip):
        def source(i):
            dest = me ^ (flip + 2 * (low + i // i_part))
            row = dest * i_block + chunk * i_part
            if i_part % 8 == 0:
                return row // 8 + (i % i_part) // 8, (i % i_part) % 8
            return row // 8, (chunk * i_part) % 8 + i % i_part

        def pairs(x, i):
            pieces = []
            for lane in range(0, lanes, 128):
                cut = slice(lane, lane + 128)
                wide, narrow = [], []
                for a in range(comps):
                    parts = []
                    for j in range(joint):
                        lead, sub = source(i + j)
                        line = turned_ref[interior[x], a, lead, sub:sub + 1, cut]
                        parts.append(jnp.broadcast_to(line, (own, 128)))
                    wide.append(jnp.concatenate(parts, 0))
                    half = wide[-1][:16].astype(BF16)
                    narrow.append(jnp.concatenate([half] * (tile // 16), 0))
                row = []
                for b in range(comps):
                    phis = wide if b == 0 else narrow
                    slope = [first_ref[x, a, :, cut] if b == 0 else grad_ref[x, b - 1, a, :, cut]
                             for a in range(comps)]
                    pair = phis[0] * slope[0]
                    for a in range(1, comps):
                        pair = pair + phis[a] * slope[a]
                    row.append(pair.astype(BF16))
                pieces.append(row)
            return [pieces[l][b] for b in range(comps) for l in range(lanes // 128)]

        total = None
        for first in range(0, len(interior), K_ROWS):
            count = min(K_ROWS, len(interior) - first)
            left = jnp.concatenate([
                jnp.concatenate([p for x in range(first, first + count) for p in pairs(x, i)], 1)
                for i in range(0, dests * i_part, joint)
            ], 0)
            right = full_ref[interior[first]:interior[first] + count].reshape(count * depth, width)
            term = jnp.dot(left, right, preferred_element_type=F32)
            total = term if total is None else total + term
        return total.reshape(dests, i_part * own, width)

    steps = halves // dests

    def step_of(step, carry):
        sends = step < steps
        low = lax.rem(step, steps) * dests
        value = group(low, jnp.where(sends, 1, 0))

        @pl.when(sends)
        def _():
            send_ref[pl.ds(low, dests), :i_part * own] = value.astype(BF16)

        @pl.when(jnp.logical_not(sends))
        def _():
            keep_ref[pl.ds(low, dests), :i_part * own] = value

        return carry

    lax.fori_loop(0, 2 * steps, step_of, 0)
    if block_rows > i_part * own:
        for low in range(halves):
            for flip, ref in ((1, send_ref), (0, keep_ref)):
                dest = me ^ (flip + 2 * low)
                rows = visc_ref[pl.ds(pl.multiple_of(dest * i_block, i_block), i_block), :]
                rows = jnp.concatenate([rows, jnp.zeros((i_block, width - own), F32)], 1)
                fill = block_rows - i_part * own - i_block
                if fill:
                    rows = jnp.concatenate([rows, jnp.zeros((fill, width), F32)], 0)
                ref[low, i_part * own:] = rows.astype(ref.dtype)


def prepare(plan, masks, cells_z, idx, sources, own):
    copies, interior, _ = plan
    rows = max(at + stop - start for _, start, stop, at in copies)
    count = sum(stop - start for start, stop in interior)
    _, comps, part, width = sources[0].shape
    lanes = part * len(masks)
    tile = max(own, 16)
    batch = max(1, min(max(stop - start for start, stop in interior), 2048 // lanes))
    return pl.pallas_call(
        functools.partial(prepare_kernel, plan, masks, cells_z, tile // own),
        out_shape=(
            jax.ShapeDtypeStruct((rows, comps, lanes, width), BF16),
            jax.ShapeDtypeStruct((rows, comps, width // 8, 8, lanes), F32),
            jax.ShapeDtypeStruct((count, comps, tile, lanes), F32),
            jax.ShapeDtypeStruct((count, comps - 1, comps, tile, lanes), BF16),
            jax.ShapeDtypeStruct((width, own), F32),
        ),
        in_specs=[SMEM] + [VMEM] * len(sources),
        out_specs=(VMEM,) * 5,
        scratch_shapes=[
            pltpu.VMEM((comps, comps, width // 8, 8, lanes), F32),
            pltpu.VMEM((width, batch * comps * comps * lanes), BF16),
            pltpu.VMEM((own, batch * comps * comps * lanes), BF16),
        ],
        compiler_params=pltpu.CompilerParams(vmem_limit_bytes=48 * 2**20),
        name="prepare",
    )(idx, *sources)


def project(plan, chunk, idx, state, own, peers):
    full, turned, first, grad, visc = state
    _, comps, lanes, width = full.shape
    halves, i_block = peers // 2, width // peers
    i_part = i_block // CHUNKS
    rows = i_part * own + (max(16, i_block) if chunk == CHUNKS - 1 else 0)
    flops = 2 * halves * 2 * i_part * own * grad.shape[0] * comps * lanes * width
    return pl.pallas_call(
        functools.partial(main_kernel, plan, own, chunk),
        out_shape=(
            jax.ShapeDtypeStruct((halves, rows, width), BF16),
            jax.ShapeDtypeStruct((halves, rows, width), F32),
        ),
        in_specs=[SMEM] + [VMEM] * 5,
        out_specs=(VMEM,) * 2,
        compiler_params=pltpu.CompilerParams(vmem_limit_bytes=48 * 2**20),
        cost_estimate=pl.CostEstimate(flops=4 * flops, bytes_accessed=4 * 2**20, transcendentals=0),
        name="project",
    )(idx, full, turned, first, grad, visc)


def body(modes):
    cells_x, cells_y, cells_z, comps, width = modes.shape
    peers_x, peers_y = lax.axis_size("gx"), lax.axis_size("gy")
    total_points = cells_x * cells_y * cells_z * peers_x * peers_y
    own = width // peers_y
    i_block = width // peers_x
    i_part = i_block // CHUNKS
    idx = jnp.stack([lax.axis_index("gy"), lax.axis_index("gx")]).astype(jnp.int32)
    block = modes.transpose(0, 3, 1, 2, 4).reshape(cells_x, comps, cells_y * cells_z, width)
    up = [(i, (i + 1) % peers_x) for i in range(peers_x)]
    down = [(j, i) for i, j in up]
    before = lax.ppermute(block[-2:], "gx", up)
    after = lax.ppermute(block[:2], "gx", down)
    padded = jnp.concatenate([before, block, after], 0)
    pieces, masks = gathered(padded, "gy")
    plan = (((0, 0, cells_x + 4, 0),), ((2, cells_x + 2),), 1)
    state = prepare(plan, masks, cells_z, idx, pieces, own)
    finals = []
    for chunk in range(CHUNKS):
        send, keep = project(plan, chunk, idx, state, own, peers_x)
        got = swap(send, "gx", 1)
        sums = keep + got.astype(F32)
        final = sums[0]
        for q in range(1, peers_x // 2):
            final = final + swap(sums[q].astype(BF16), "gx", 2 * q).astype(F32)
        finals.append(final)
    convective = jnp.concatenate(
        [f[:i_part * own].reshape(i_part, own, width) for f in finals], 0
    ) * (-1.0 / math.sqrt(total_points))
    viscous = finals[-1][i_part * own:i_part * own + i_block, :own] * (-1.0 / total_points)
    return (convective, viscous)


def solution(mesh):
    in_specs = (P("gx", "gy", None, None, None),)
    out_specs = (P("gx", "gy", None), P("gx", "gy"))
    return jax.shard_map(body, mesh=mesh, in_specs=in_specs, out_specs=out_specs, check_vma=False)
```

```python
import functools
import math

import jax
import jax.numpy as jnp
from jax import lax
from jax.experimental import pallas as pl
from jax.experimental.pallas import tpu as pltpu
from jax.sharding import PartitionSpec as P

BF16, F32 = jnp.bfloat16, jnp.float32
VMEM = pl.BlockSpec(memory_space=pltpu.VMEM)
SMEM = pl.BlockSpec(memory_space=pltpu.SMEM)
CHUNKS = 2
K_ROWS = 4


def group_rows(lanes):
    return 32 if lanes <= 128 else 16


def vmem_limit(lanes):
    return min(52, 16 * -(-lanes // 128)) * 2**20


def swap(x, axis, mask):
    return lax.ppermute(x, axis, [(i, i ^ mask) for i in range(lax.axis_size(axis))])


def gathered(x, axis):
    pieces, mask = [x], lax.axis_size(axis) // 2
    masks = [0]
    while mask:
        pieces += [swap(piece, axis, mask) for piece in pieces]
        masks += [m ^ mask for m in masks]
        mask //= 2
    return pieces, masks


def gathered_stack(x, axis):
    stack, mask = x[None], lax.axis_size(axis) // 2
    while mask:
        stack = jnp.concatenate([stack, swap(stack, axis, mask)], 0)
        mask //= 2
    return stack


def y_and_z_weights(lanes, cells_z):
    q = lax.broadcasted_iota(jnp.int32, (lanes, lanes), 0)
    p = lax.broadcasted_iota(jnp.int32, (lanes, lanes), 1)
    apart = q - p
    around = jnp.where(apart < 0, apart + lanes, apart)
    same = lax.div(q, cells_z) == lax.div(p, cells_z)
    weights_y = jnp.zeros((lanes, lanes), F32)
    weights_z = jnp.zeros((lanes, lanes), F32)
    for step, weight in ((1, 8.0), (-1, -8.0), (2, -1.0), (-2, 1.0)):
        weights_y = weights_y + jnp.where(around == (step * cells_z) % lanes, weight, 0.0)
        weights_z = weights_z + jnp.where(same & (apart == step), weight, 0.0)
    return jnp.concatenate([weights_y, weights_z], 1).astype(BF16)


def prepare_kernel(plan, masks, cells_z, repeat, idx_ref, *refs):
    copies, interior = plan
    pieces = len(masks)
    edges_ref = refs[pieces]
    sources = (refs[:pieces], [edges_ref.at[q] for q in range(pieces)])
    full_ref, turned_ref, first_ref, grad_ref, visc_ref, slope_ref, every_ref, mine_ref = refs[pieces + 1:]
    rows, comps, lanes, width = full_ref.shape
    part = lanes // pieces
    me = idx_ref[0]
    own = width // pieces
    for q, mask in enumerate(masks):
        slot = pl.multiple_of((me ^ mask) * part, part)
        for source, start, stop, at in copies:
            full_ref[at:at + stop - start, :, pl.ds(slot, part), :] = sources[source][q][start:stop]

    def turn(row, carry):
        for comp in range(comps):
            flat = full_ref[row, comp].astype(F32).T
            turned_ref[row, comp] = flat.reshape(width // 8, 8, lanes)
        return carry

    lax.fori_loop(0, rows, turn, 0, unroll=4)
    weights = y_and_z_weights(lanes, cells_z)

    def slopes(at, slot, row):
        mine, every = [], []
        for comp in range(comps):
            def line(step):
                return turned_ref[row + step, comp].reshape(width, lanes)

            along_x = (8.0 * (line(1) - line(-1)) - (line(2) - line(-2))) * (1.0 / 12.0)
            others = jnp.dot(line(0).astype(BF16), weights, preferred_element_type=F32) * (1.0 / 12.0)
            for b, value in enumerate((along_x, others[:, :lanes], others[:, lanes:])):
                slope_ref[b, comp] = value.reshape(width // 8, 8, lanes)
                every.append(value.astype(BF16))
        for b in range(comps):
            for comp in range(comps):
                block = slope_ref[b, comp, pl.ds(me * (own // 8), own // 8)].reshape(own, lanes).astype(BF16)
                mine.append((b, comp, block))
                tiled = jnp.concatenate([block] * repeat, 0)
                if b == 0:
                    first_ref[at, comp] = tiled.astype(F32)
                else:
                    grad_ref[at, b - 1, comp] = tiled
        mine = [m[2] for m in sorted(mine, key=lambda m: (m[1], m[0]))]
        column = pl.ds(pl.multiple_of(slot * (comps * comps * lanes), lanes), comps * comps * lanes)
        every_ref[:, column] = jnp.concatenate(every, 1)
        mine_ref[:, column] = jnp.concatenate(mine, 1)

    batch = mine_ref.shape[1] // (comps * comps * lanes)
    steps = [(row, min(row + batch, stop)) for start, stop in interior for row in range(start, stop, batch)]
    at = 0
    for start, stop in steps:
        def one(step, carry, start=start, at=at):
            slopes(at + step, step, start + step)
            return carry

        lax.fori_loop(0, stop - start, one, 0, unroll=4)
        used = (stop - start) * comps * comps * lanes
        term = lax.dot_general(
            every_ref[:, :used], mine_ref[:, :used], (((1,), (1,)), ((), ())), preferred_element_type=F32
        )
        visc_ref[...] = term if at == 0 else visc_ref[...] + term
        at += stop - start


def main_kernel(plan, own, chunk, idx_ref, full_ref, turned_ref, first_ref, grad_ref, visc_ref,
                send_ref, keep_ref):
    interior = [r for start, stop in plan[1] for r in range(start, stop)]
    _, comps, lanes, width = full_ref.shape
    halves, block_rows = send_ref.shape[:2]
    peers = 2 * halves
    i_block = width // peers
    i_part = i_block // CHUNKS
    tile = grad_ref.shape[3]
    joint = tile // own
    me = idx_ref[1]
    depth = comps * lanes
    dests = max(1, min(halves, group_rows(lanes) // i_part))

    def group(low, flip):
        def source(i):
            dest = me ^ (flip + 2 * (low + i // i_part))
            row = dest * i_block + chunk * i_part
            if i_part % 8 == 0:
                return row // 8 + (i % i_part) // 8, (i % i_part) % 8
            return row // 8, (chunk * i_part) % 8 + i % i_part

        def pairs(x, i):
            pieces = []
            for lane in range(0, lanes, 128):
                cut = slice(lane, lane + 128)
                wide, narrow = [], []
                for a in range(comps):
                    parts = []
                    for j in range(joint):
                        lead, sub = source(i + j)
                        line = turned_ref[interior[x], a, lead, sub:sub + 1, cut]
                        parts.append(jnp.broadcast_to(line, (own, 128)))
                    wide.append(jnp.concatenate(parts, 0))
                    half = wide[-1][:16].astype(BF16)
                    narrow.append(jnp.concatenate([half] * (tile // 16), 0))
                row = []
                for b in range(comps):
                    phis = wide if b == 0 else narrow
                    slope = [first_ref[x, a, :, cut] if b == 0 else grad_ref[x, b - 1, a, :, cut]
                             for a in range(comps)]
                    pair = phis[0] * slope[0]
                    for a in range(1, comps):
                        pair = pair + phis[a] * slope[a]
                    row.append(pair.astype(BF16))
                pieces.append(row)
            return [pieces[l][b] for b in range(comps) for l in range(lanes // 128)]

        total = None
        for first in range(0, len(interior), K_ROWS):
            count = min(K_ROWS, len(interior) - first)
            left = jnp.concatenate([
                jnp.concatenate([p for x in range(first, first + count) for p in pairs(x, i)], 1)
                for i in range(0, dests * i_part, joint)
            ], 0)
            right = full_ref[interior[first]:interior[first] + count].reshape(count * depth, width)
            term = jnp.dot(left, right, preferred_element_type=F32)
            total = term if total is None else total + term
        return total.reshape(dests, i_part * own, width)

    steps = halves // dests

    def step_of(step, carry):
        sends = step < steps
        low = lax.rem(step, steps) * dests
        value = group(low, jnp.where(sends, 1, 0))

        @pl.when(sends)
        def _():
            send_ref[pl.ds(low, dests), :i_part * own] = value.astype(BF16)

        @pl.when(jnp.logical_not(sends))
        def _():
            keep_ref[pl.ds(low, dests), :i_part * own] = value

        return carry

    lax.fori_loop(0, 2 * steps, step_of, 0)
    if block_rows > i_part * own:
        for low in range(halves):
            for flip, ref in ((1, send_ref), (0, keep_ref)):
                dest = me ^ (flip + 2 * low)
                rows = visc_ref[pl.ds(pl.multiple_of(dest * i_block, i_block), i_block), :]
                rows = jnp.concatenate([rows, jnp.zeros((i_block, width - own), F32)], 1)
                fill = block_rows - i_part * own - i_block
                if fill:
                    rows = jnp.concatenate([rows, jnp.zeros((fill, width), F32)], 0)
                ref[low, i_part * own:] = rows.astype(ref.dtype)


def prepare(plan, masks, cells_z, idx, sources, edges, own):
    copies, interior = plan
    rows = max(at + stop - start for _, start, stop, at in copies)
    count = sum(stop - start for start, stop in interior)
    _, comps, part, width = sources[0].shape
    lanes = part * len(masks)
    tile = max(own, 16)
    batch = max(1, min(max(stop - start for start, stop in interior), 2048 // lanes))
    return pl.pallas_call(
        functools.partial(prepare_kernel, plan, masks, cells_z, tile // own),
        out_shape=(
            jax.ShapeDtypeStruct((rows, comps, lanes, width), BF16),
            jax.ShapeDtypeStruct((rows, comps, width // 8, 8, lanes), F32),
            jax.ShapeDtypeStruct((count, comps, tile, lanes), F32),
            jax.ShapeDtypeStruct((count, comps - 1, comps, tile, lanes), BF16),
            jax.ShapeDtypeStruct((width, own), F32),
        ),
        in_specs=[SMEM] + [VMEM] * (len(sources) + 1),
        out_specs=(VMEM,) * 5,
        scratch_shapes=[
            pltpu.VMEM((comps, comps, width // 8, 8, lanes), F32),
            pltpu.VMEM((width, batch * comps * comps * lanes), BF16),
            pltpu.VMEM((own, batch * comps * comps * lanes), BF16),
        ],
        compiler_params=pltpu.CompilerParams(vmem_limit_bytes=vmem_limit(lanes)),
        name="prepare",
    )(idx, *sources, edges)


def project(plan, chunk, idx, state, own, peers):
    full, turned, first, grad, visc = state
    _, comps, lanes, width = full.shape
    halves, i_block = peers // 2, width // peers
    i_part = i_block // CHUNKS
    rows = i_part * own + (max(16, i_block) if chunk == CHUNKS - 1 else 0)
    flops = 2 * halves * 2 * i_part * own * grad.shape[0] * comps * lanes * width
    return pl.pallas_call(
        functools.partial(main_kernel, plan, own, chunk),
        out_shape=(
            jax.ShapeDtypeStruct((halves, rows, width), BF16),
            jax.ShapeDtypeStruct((halves, rows, width), F32),
        ),
        in_specs=[SMEM] + [VMEM] * 5,
        out_specs=(VMEM,) * 2,
        compiler_params=pltpu.CompilerParams(vmem_limit_bytes=vmem_limit(lanes)),
        cost_estimate=pl.CostEstimate(flops=4 * flops, bytes_accessed=4 * 2**20, transcendentals=0),
        name="project",
    )(idx, full, turned, first, grad, visc)


def body(modes):
    cells_x, cells_y, cells_z, comps, width = modes.shape
    peers_x, peers_y = lax.axis_size("gx"), lax.axis_size("gy")
    total_points = cells_x * cells_y * cells_z * peers_x * peers_y
    own = width // peers_y
    i_block = width // peers_x
    i_part = i_block // CHUNKS
    idx = jnp.stack([lax.axis_index("gy"), lax.axis_index("gx")]).astype(jnp.int32)
    block = modes.transpose(0, 3, 1, 2, 4).reshape(cells_x, comps, cells_y * cells_z, width)
    up = [(i, (i + 1) % peers_x) for i in range(peers_x)]
    down = [(j, i) for i, j in up]
    pieces, masks = gathered(block, "gy")
    before = lax.ppermute(block[-2:], "gx", up)
    after = lax.ppermute(block[:2], "gx", down)
    edges = gathered_stack(jnp.concatenate([before, after], 0), "gy")
    plan = (
        ((0, 0, cells_x, 2), (1, 0, 2, 0), (1, 2, 4, cells_x + 2)),
        ((2, cells_x + 2),),
    )
    state = prepare(plan, masks, cells_z, idx, pieces, edges, own)
    finals = []
    for chunk in range(CHUNKS):
        send, keep = project(plan, chunk, idx, state, own, peers_x)
        got = swap(send, "gx", 1)
        sums = keep + got.astype(F32)
        final = sums[0]
        for q in range(1, peers_x // 2):
            final = final + swap(sums[q].astype(BF16), "gx", 2 * q).astype(F32)
        finals.append(final)
    convective = jnp.concatenate(
        [f[:i_part * own].reshape(i_part, own, width) for f in finals], 0
    ) * (-1.0 / math.sqrt(total_points))
    viscous = finals[-1][i_part * own:i_part * own + i_block, :own] * (-1.0 / total_points)
    return (convective, viscous)


def solution(mesh):
    in_specs = (P("gx", "gy", None, None, None),)
    out_specs = (P("gx", "gy", None), P("gx", "gy"))
    return jax.shard_map(body, mesh=mesh, in_specs=in_specs, out_specs=out_specs, check_vma=False)
```

```python
import functools
import math

import jax
import jax.numpy as jnp
from jax import lax
from jax.experimental import pallas as pl
from jax.experimental.pallas import tpu as pltpu
from jax.sharding import PartitionSpec as P

BF16, F32 = jnp.bfloat16, jnp.float32
VMEM = pl.BlockSpec(memory_space=pltpu.VMEM)
SMEM = pl.BlockSpec(memory_space=pltpu.SMEM)
PARTS = 2
K_ROWS = 4


def group_rows(lanes):
    return 32 if lanes <= 128 else 8


def vmem_limit(lanes):
    return min(52, 16 * -(-lanes // 128)) * 2**20


def swap(x, axis, mask):
    return lax.ppermute(x, axis, [(i, i ^ mask) for i in range(lax.axis_size(axis))])


def gathered(x, axis):
    pieces, mask = [x], lax.axis_size(axis) // 2
    masks = [0]
    while mask:
        pieces += [swap(piece, axis, mask) for piece in pieces]
        masks += [m ^ mask for m in masks]
        mask //= 2
    return pieces, masks


def gathered_stack(x, axis):
    stack, mask = x[None], lax.axis_size(axis) // 2
    while mask:
        stack = jnp.concatenate([stack, swap(stack, axis, mask)], 0)
        mask //= 2
    return stack


def y_and_z_weights(lanes, cells_z):
    q = lax.broadcasted_iota(jnp.int32, (lanes, lanes), 0)
    p = lax.broadcasted_iota(jnp.int32, (lanes, lanes), 1)
    apart = q - p
    around = jnp.where(apart < 0, apart + lanes, apart)
    same = lax.div(q, cells_z) == lax.div(p, cells_z)
    weights_y = jnp.zeros((lanes, lanes), F32)
    weights_z = jnp.zeros((lanes, lanes), F32)
    for step, weight in ((1, 8.0), (-1, -8.0), (2, -1.0), (-2, 1.0)):
        weights_y = weights_y + jnp.where(around == (step * cells_z) % lanes, weight, 0.0)
        weights_z = weights_z + jnp.where(same & (apart == step), weight, 0.0)
    return jnp.concatenate([weights_y, weights_z], 1).astype(BF16)


def prepare_kernel(plan, masks, cells_z, repeat, idx_ref, *refs):
    copies, interior = plan
    pieces = len(masks)
    edges_ref = refs[pieces]
    sources = (refs[:pieces], [edges_ref.at[q] for q in range(pieces)])
    full_ref, turned_ref, first_ref, grad_ref, visc_ref, slope_ref, every_ref, mine_ref = refs[pieces + 1:]
    rows, comps, lanes, width = full_ref.shape
    part = lanes // pieces
    me = idx_ref[0]
    own = width // pieces
    for q, mask in enumerate(masks):
        slot = pl.multiple_of((me ^ mask) * part, part)
        for source, start, stop, at in copies:
            full_ref[at:at + stop - start, :, pl.ds(slot, part), :] = sources[source][q][start:stop]

    def turn(row, carry):
        for comp in range(comps):
            flat = full_ref[row, comp].astype(F32).T
            turned_ref[row, comp] = flat.reshape(width // 8, 8, lanes)
        return carry

    lax.fori_loop(0, rows, turn, 0, unroll=4)
    weights = y_and_z_weights(lanes, cells_z)

    def slopes(at, slot, row):
        mine, every = [], []
        for comp in range(comps):
            def line(step):
                return turned_ref[row + step, comp].reshape(width, lanes)

            along_x = (8.0 * (line(1) - line(-1)) - (line(2) - line(-2))) * (1.0 / 12.0)
            others = jnp.dot(line(0).astype(BF16), weights, preferred_element_type=F32) * (1.0 / 12.0)
            for b, value in enumerate((along_x, others[:, :lanes], others[:, lanes:])):
                slope_ref[b, comp] = value.reshape(width // 8, 8, lanes)
                every.append(value.astype(BF16))
        for b in range(comps):
            for comp in range(comps):
                block = slope_ref[b, comp, pl.ds(me * (own // 8), own // 8)].reshape(own, lanes).astype(BF16)
                mine.append((b, comp, block))
                tiled = jnp.concatenate([block] * repeat, 0)
                if b == 0:
                    first_ref[at, comp] = tiled.astype(F32)
                else:
                    grad_ref[at, b - 1, comp] = tiled
        mine = [m[2] for m in sorted(mine, key=lambda m: (m[1], m[0]))]
        column = pl.ds(pl.multiple_of(slot * (comps * comps * lanes), lanes), comps * comps * lanes)
        every_ref[:, column] = jnp.concatenate(every, 1)
        mine_ref[:, column] = jnp.concatenate(mine, 1)

    batch = mine_ref.shape[1] // (comps * comps * lanes)
    steps = [(row, min(row + batch, stop)) for start, stop in interior for row in range(start, stop, batch)]
    at = 0
    for start, stop in steps:
        def one(step, carry, start=start, at=at):
            slopes(at + step, step, start + step)
            return carry

        lax.fori_loop(0, stop - start, one, 0, unroll=4)
        used = (stop - start) * comps * comps * lanes
        term = lax.dot_general(
            every_ref[:, :used], mine_ref[:, :used], (((1,), (1,)), ((), ())), preferred_element_type=F32
        )
        visc_ref[...] = term if at == 0 else visc_ref[...] + term
        at += stop - start


def code_of(part, stage, j):
    if part == 0 or stage >= 2:
        return (2 * j + 1) << stage
    if stage == 0:
        return (j & 1) | 2 | ((j >> 1) << 2)
    return 1 | (j << 2)


def bit_of(part, stage):
    return 1 - stage if part == 1 and stage < 2 else stage


def main_kernel(plan, own, stage, parts, idx_ref, full_ref, turned_ref, first_ref, grad_ref, visc_ref, *out_refs):
    interior = [r for start, stop in plan[1] for r in range(start, stop)]
    _, comps, lanes, width = full_ref.shape
    i_block, i_part = parts[0][2], parts[0][3]
    tile = grad_ref.shape[3]
    joint = tile // own
    me = idx_ref[1]
    depth = comps * lanes

    def code(part, j):
        return 0 if stage is None else code_of(part, stage, j)

    def group(jobs):
        def source(i):
            part, j = jobs[i // i_part]
            row = (me ^ code(part, j)) * i_block + part * i_part
            if i_part % 8 == 0:
                return row // 8 + (i % i_part) // 8, i % 8
            return row // 8, (part * i_part) % 8 + i % i_part

        def pairs(x, i):
            pieces = []
            for lane in range(0, lanes, 128):
                cut = slice(lane, lane + 128)
                wide, narrow = [], []
                for a in range(comps):
                    lines = []
                    for j in range(joint):
                        lead, sub = source(i + j)
                        line = turned_ref[interior[x], a, lead, sub:sub + 1, cut]
                        lines.append(jnp.broadcast_to(line, (own, 128)))
                    wide.append(jnp.concatenate(lines, 0))
                    half = wide[-1][:16].astype(BF16)
                    narrow.append(jnp.concatenate([half] * (tile // 16), 0))
                row = []
                for b in range(comps):
                    phis = wide if b == 0 else narrow
                    slope = [first_ref[x, a, :, cut] if b == 0 else grad_ref[x, b - 1, a, :, cut]
                             for a in range(comps)]
                    pair = phis[0] * slope[0]
                    for a in range(1, comps):
                        pair = pair + phis[a] * slope[a]
                    row.append(pair.astype(BF16))
                pieces.append(row)
            return [pieces[l][b] for b in range(comps) for l in range(lanes // 128)]

        total = None
        for first in range(0, len(interior), K_ROWS):
            count = min(K_ROWS, len(interior) - first)
            left = jnp.concatenate([
                jnp.concatenate([p for x in range(first, first + count) for p in pairs(x, i)], 1)
                for i in range(0, len(jobs) * i_part, joint)
            ], 0)
            right = full_ref[interior[first]:interior[first] + count].reshape(count * depth, width)
            term = jnp.dot(left, right, preferred_element_type=F32)
            total = term if total is None else total + term
        return total.reshape(len(jobs), i_part * own, width)

    jobs = [(part, j) for part, count, _, _ in parts for j in range(count)]
    at_once = group_rows(lanes) // i_part
    if len(jobs) <= at_once:
        value, at = group(jobs), 0
        for (part, count, _, _), ref in zip(parts, out_refs):
            ref[:, :i_part * own] = value[at:at + count].astype(ref.dtype)
            at += count
    else:
        for (part, count, _, _), ref in zip(parts, out_refs):
            size = min(at_once, count)

            def one(step, carry, part=part, ref=ref, size=size):
                low = step * size
                value = group([(part, low + j) for j in range(size)])
                ref[pl.ds(low, size), :i_part * own] = value.astype(ref.dtype)
                return carry

            lax.fori_loop(0, count // size, one, 0)
    for (part, count, _, _), ref in zip(parts, out_refs):
        if part == 0:
            for j in range(count):
                dest = me ^ code(part, j)
                rows = visc_ref[pl.ds(pl.multiple_of(dest * i_block, i_block), i_block), :]
                rows = jnp.concatenate([rows, jnp.zeros((i_block, width - own), F32)], 1)
                fill = ref.shape[1] - i_part * own - i_block
                if fill:
                    rows = jnp.concatenate([rows, jnp.zeros((fill, width), F32)], 0)
                ref[j, i_part * own:] = rows.astype(ref.dtype)


def prepare(plan, masks, cells_z, idx, sources, edges, own):
    copies, interior = plan
    rows = max(at + stop - start for _, start, stop, at in copies)
    count = sum(stop - start for start, stop in interior)
    _, comps, part, width = sources[0].shape
    lanes = part * len(masks)
    tile = max(own, 16)
    batch = max(1, min(max(stop - start for start, stop in interior), 2048 // lanes))
    return pl.pallas_call(
        functools.partial(prepare_kernel, plan, masks, cells_z, tile // own),
        out_shape=(
            jax.ShapeDtypeStruct((rows, comps, lanes, width), BF16),
            jax.ShapeDtypeStruct((rows, comps, width // 8, 8, lanes), F32),
            jax.ShapeDtypeStruct((count, comps, tile, lanes), F32),
            jax.ShapeDtypeStruct((count, comps - 1, comps, tile, lanes), BF16),
            jax.ShapeDtypeStruct((width, own), F32),
        ),
        in_specs=[SMEM] + [VMEM] * (len(sources) + 1),
        out_specs=(VMEM,) * 5,
        scratch_shapes=[
            pltpu.VMEM((comps, comps, width // 8, 8, lanes), F32),
            pltpu.VMEM((width, batch * comps * comps * lanes), BF16),
            pltpu.VMEM((own, batch * comps * comps * lanes), BF16),
        ],
        compiler_params=pltpu.CompilerParams(vmem_limit_bytes=vmem_limit(lanes)),
        name="prepare",
    )(idx, *sources, edges)


def project(plan, stage, parts, idx, state, own, peers, dtype):
    full, turned, first, grad, visc = state
    _, comps, lanes, width = full.shape
    i_block = width // peers
    i_part = i_block // PARTS
    count = 1 if stage is None else peers >> (stage + 1)
    sizes = [i_part * own + (max(16, i_block) if part == 0 else 0) for part in parts]
    flops = 2 * len(parts) * count * i_part * own * grad.shape[0] * comps * lanes * width
    return pl.pallas_call(
        functools.partial(main_kernel, plan, own, stage, [(part, count, i_block, i_part) for part in parts]),
        out_shape=[jax.ShapeDtypeStruct((count, rows, width), dtype) for rows in sizes],
        in_specs=[SMEM] + [VMEM] * 5,
        out_specs=[VMEM] * len(parts),
        compiler_params=pltpu.CompilerParams(vmem_limit_bytes=vmem_limit(lanes)),
        cost_estimate=pl.CostEstimate(flops=4 * flops, bytes_accessed=2**20, transcendentals=0),
        name="project",
    )(idx, full, turned, first, grad, visc)


def arrived(results, part, code):
    found = []
    for stage, blocks in enumerate(results):
        for j in range(blocks.shape[0]):
            if code_of(part, stage, j) ^ (1 << bit_of(part, stage)) == code:
                found.append(blocks[j].astype(F32))
    return sum(found)


def body(modes):
    cells_x, cells_y, cells_z, comps, width = modes.shape
    peers_x, peers_y = lax.axis_size("gx"), lax.axis_size("gy")
    total_points = cells_x * cells_y * cells_z * peers_x * peers_y
    own = width // peers_y
    i_block = width // peers_x
    i_part = i_block // PARTS
    idx = jnp.stack([lax.axis_index("gy"), lax.axis_index("gx")]).astype(jnp.int32)
    block = modes.transpose(0, 3, 1, 2, 4).reshape(cells_x, comps, cells_y * cells_z, width)
    up = [(i, (i + 1) % peers_x) for i in range(peers_x)]
    down = [(j, i) for i, j in up]
    pieces, masks = gathered(block, "gy")
    before = lax.ppermute(block[-2:], "gx", up)
    after = lax.ppermute(block[:2], "gx", down)
    edges = gathered_stack(jnp.concatenate([before, after], 0), "gy")
    plan = (
        ((0, 0, cells_x, 2), (1, 0, 2, 0), (1, 2, 4, cells_x + 2)),
        ((2, cells_x + 2),),
    )
    state = prepare(plan, masks, cells_z, idx, pieces, edges, own)
    stages = peers_x.bit_length() - 1
    both = tuple(range(PARTS))
    results = [[], []]
    for part in both:
        (send,) = project(plan, 0, (part,), idx, state, own, peers_x, BF16)
        results[part].append(swap(send, "gx", 1 << bit_of(part, 0)))
        idx, send = lax.optimization_barrier((idx, send))
    for stage in range(1, stages):
        kept = project(plan, stage, both, idx, state, own, peers_x, F32)
        sums = [
            jnp.stack([kept[part][j] + arrived(results[part], part, code_of(part, stage, j))
                       for j in range(kept[part].shape[0])]).astype(BF16)
            for part in both
        ]
        if bit_of(0, stage) == bit_of(1, stage):
            rows = sums[0].shape[1]
            joined = swap(jnp.concatenate(sums, 1), "gx", 1 << stage)
            got = [joined[:, :rows], joined[:, rows:]]
        else:
            got = [swap(sums[part], "gx", 1 << bit_of(part, stage)) for part in both]
        for part in both:
            results[part].append(got[part])
        idx, sums = lax.optimization_barrier((idx, sums))
    kept = project(plan, None, both, idx, state, own, peers_x, F32)
    finals = [kept[part][0] + arrived(results[part], part, 0) for part in both]
    convective = jnp.concatenate(
        [f[:i_part * own].reshape(i_part, own, width) for f in finals], 0
    ) * (-1.0 / math.sqrt(total_points))
    viscous = finals[0][i_part * own:i_part * own + i_block, :own] * (-1.0 / total_points)
    return (convective, viscous)


def solution(mesh):
    in_specs = (P("gx", "gy", None, None, None),)
    out_specs = (P("gx", "gy", None), P("gx", "gy"))
    return jax.shard_map(body, mesh=mesh, in_specs=in_specs, out_specs=out_specs, check_vma=False)
```

```python
import functools
import math

import jax
import jax.numpy as jnp
from jax import lax
from jax.experimental import pallas as pl
from jax.experimental.pallas import tpu as pltpu
from jax.sharding import PartitionSpec as P

BF16, F32 = jnp.bfloat16, jnp.float32
VMEM = pl.BlockSpec(memory_space=pltpu.VMEM)
SMEM = pl.BlockSpec(memory_space=pltpu.SMEM)
PARTS = 2
K_ROWS = 4


def group_rows(lanes):
    return 32 if lanes <= 128 else 8


def vmem_limit(lanes):
    return min(52, 16 * -(-lanes // 128)) * 2**20


def swap(x, axis, mask):
    return lax.ppermute(x, axis, [(i, i ^ mask) for i in range(lax.axis_size(axis))])


def gathered(x, axis):
    pieces, mask = [x], lax.axis_size(axis) // 2
    masks = [0]
    while mask:
        pieces += [swap(piece, axis, mask) for piece in pieces]
        masks += [m ^ mask for m in masks]
        mask //= 2
    return pieces, masks


def gathered_stack(x, axis, behind):
    stack, mask = x[None], lax.axis_size(axis) // 2
    while mask:
        got = swap(stack, axis, mask)
        if behind is not None:
            stack, got, behind = *lax.optimization_barrier((stack, got, behind))[:2], None
        stack = jnp.concatenate([stack, got], 0)
        mask //= 2
    return stack


def y_and_z_weights(lanes, cells_z):
    q = lax.broadcasted_iota(jnp.int32, (lanes, lanes), 0)
    p = lax.broadcasted_iota(jnp.int32, (lanes, lanes), 1)
    apart = q - p
    around = jnp.where(apart < 0, apart + lanes, apart)
    same = lax.div(q, cells_z) == lax.div(p, cells_z)
    weights_y = jnp.zeros((lanes, lanes), F32)
    weights_z = jnp.zeros((lanes, lanes), F32)
    for step, weight in ((1, 8.0), (-1, -8.0), (2, -1.0), (-2, 1.0)):
        weights_y = weights_y + jnp.where(around == (step * cells_z) % lanes, weight, 0.0)
        weights_z = weights_z + jnp.where(same & (apart == step), weight, 0.0)
    return jnp.concatenate([weights_y, weights_z], 1).astype(BF16)


def prepare_kernel(plan, masks, cells_z, repeat, idx_ref, *refs):
    copies, interior = plan
    pieces = len(masks)
    extra = 1 if any(source for source, *_ in copies) else 0
    sources = [refs[:pieces]]
    if extra:
        sources.append([refs[pieces].at[q] for q in range(pieces)])
    full_ref, turned_ref, first_ref, grad_ref, visc_ref, slope_ref, every_ref, mine_ref = refs[pieces + extra:]
    rows, comps, lanes, width = full_ref.shape
    part = lanes // pieces
    me = idx_ref[0]
    own = width // pieces
    for q, mask in enumerate(masks):
        slot = pl.multiple_of((me ^ mask) * part, part)
        for source, start, stop, at in copies:
            full_ref[at:at + stop - start, :, pl.ds(slot, part), :] = sources[source][q][start:stop]

    def turn(row, carry):
        for comp in range(comps):
            flat = full_ref[row, comp].astype(F32).T
            turned_ref[row, comp] = flat.reshape(width // 8, 8, lanes)
        return carry

    lax.fori_loop(0, rows, turn, 0, unroll=4)
    weights = y_and_z_weights(lanes, cells_z)

    def slopes(at, slot, row):
        mine, every = [], []
        for comp in range(comps):
            def line(step):
                return turned_ref[row + step, comp].reshape(width, lanes)

            along_x = (8.0 * (line(1) - line(-1)) - (line(2) - line(-2))) * (1.0 / 12.0)
            others = jnp.dot(line(0).astype(BF16), weights, preferred_element_type=F32) * (1.0 / 12.0)
            for b, value in enumerate((along_x, others[:, :lanes], others[:, lanes:])):
                slope_ref[b, comp] = value.reshape(width // 8, 8, lanes)
                every.append(value.astype(BF16))
        for b in range(comps):
            for comp in range(comps):
                block = slope_ref[b, comp, pl.ds(me * (own // 8), own // 8)].reshape(own, lanes).astype(BF16)
                mine.append((b, comp, block))
                tiled = jnp.concatenate([block] * repeat, 0)
                if b == 0:
                    first_ref[at, comp] = tiled.astype(F32)
                else:
                    grad_ref[at, b - 1, comp] = tiled
        mine = [m[2] for m in sorted(mine, key=lambda m: (m[1], m[0]))]
        column = pl.ds(pl.multiple_of(slot * (comps * comps * lanes), lanes), comps * comps * lanes)
        every_ref[:, column] = jnp.concatenate(every, 1)
        mine_ref[:, column] = jnp.concatenate(mine, 1)

    batch = mine_ref.shape[1] // (comps * comps * lanes)
    steps = [(row, min(row + batch, stop)) for start, stop in interior for row in range(start, stop, batch)]
    at = 0
    for start, stop in steps:
        def one(step, carry, start=start, at=at):
            slopes(at + step, step, start + step)
            return carry

        lax.fori_loop(0, stop - start, one, 0, unroll=4)
        used = (stop - start) * comps * comps * lanes
        term = lax.dot_general(
            every_ref[:, :used], mine_ref[:, :used], (((1,), (1,)), ((), ())), preferred_element_type=F32
        )
        visc_ref[...] = term if at == 0 else visc_ref[...] + term
        at += stop - start


def code_of(part, stage, j):
    if part == 0 or stage >= 2:
        return (2 * j + 1) << stage
    if stage == 0:
        return (j & 1) | 2 | ((j >> 1) << 2)
    return 1 | (j << 2)


def bit_of(part, stage):
    return 1 - stage if part == 1 and stage < 2 else stage


def main_kernel(plans, own, stage, parts, prior, viscous, earlier, idx_ref, *refs):
    states = [refs[5 * n:5 * n + 5] for n in range(len(plans))]
    prior_refs = refs[5 * len(plans):5 * len(plans) + (len(parts) if prior else 0)]
    out_refs = refs[len(refs) - len(parts):]
    visc_refs = [state[4] for state in states] + list(refs[len(refs) - len(parts) - earlier:len(refs) - len(parts)])
    rows_of = [[r for start, stop in plan[1] for r in range(start, stop)] for plan in plans]
    _, comps, lanes, width = states[0][0].shape
    i_block, i_part = parts[0][2], parts[0][3]
    tile = states[0][3].shape[3]
    joint = tile // own
    me = idx_ref[1]
    depth = comps * lanes

    def code(part, j):
        return 0 if stage is None else code_of(part, stage, j)

    def group(jobs):
        def source(i):
            part, j = jobs[i // i_part]
            row = (me ^ code(part, j)) * i_block + part * i_part
            if i_part % 8 == 0:
                return row // 8 + (i % i_part) // 8, i % 8
            return row // 8, (part * i_part) % 8 + i % i_part

        def pairs(state, interior, x, i):
            _, turned_ref, first_ref, grad_ref, _ = state
            pieces = []
            for lane in range(0, lanes, 128):
                cut = slice(lane, lane + 128)
                wide, narrow = [], []
                for a in range(comps):
                    lines = []
                    for j in range(joint):
                        lead, sub = source(i + j)
                        line = turned_ref[interior[x], a, lead, sub:sub + 1, cut]
                        lines.append(jnp.broadcast_to(line, (own, 128)))
                    wide.append(jnp.concatenate(lines, 0))
                    half = wide[-1][:16].astype(BF16)
                    narrow.append(jnp.concatenate([half] * (tile // 16), 0))
                row = []
                for b in range(comps):
                    phis = wide if b == 0 else narrow
                    slope = [first_ref[x, a, :, cut] if b == 0 else grad_ref[x, b - 1, a, :, cut]
                             for a in range(comps)]
                    pair = phis[0] * slope[0]
                    for a in range(1, comps):
                        pair = pair + phis[a] * slope[a]
                    row.append(pair.astype(BF16))
                pieces.append(row)
            return [pieces[l][b] for b in range(comps) for l in range(lanes // 128)]

        total = None
        for state, interior in zip(states, rows_of):
            for first in range(0, len(interior), K_ROWS):
                count = min(K_ROWS, len(interior) - first)
                left = jnp.concatenate([
                    jnp.concatenate(
                        [p for x in range(first, first + count) for p in pairs(state, interior, x, i)], 1
                    )
                    for i in range(0, len(jobs) * i_part, joint)
                ], 0)
                right = state[0][interior[first]:interior[first] + count].reshape(count * depth, width)
                term = jnp.dot(left, right, preferred_element_type=F32)
                total = term if total is None else total + term
        return total.reshape(len(jobs), i_part * own, width)

    jobs = [(part, j) for part, count, _, _ in parts for j in range(count)]
    at_once = group_rows(lanes) // i_part

    def put(n, low, value):
        if prior:
            value = value + prior_refs[n][pl.ds(low, value.shape[0])]
        out_refs[n][pl.ds(low, value.shape[0]), :i_part * own] = value.astype(out_refs[n].dtype)

    if len(jobs) <= at_once:
        value, at = group(jobs), 0
        for n, (_, count, _, _) in enumerate(parts):
            put(n, 0, value[at:at + count])
            at += count
    else:
        for n, (part, count, _, _) in enumerate(parts):
            size = min(at_once, count)

            def one(step, carry, n=n, part=part, size=size):
                low = step * size
                put(n, low, group([(part, low + j) for j in range(size)]))
                return carry

            lax.fori_loop(0, count // size, one, 0)
    for (part, count, _, _), out_ref in zip(parts, out_refs):
        if part == 0 and viscous:
            for j in range(count):
                dest = me ^ code(part, j)
                block = pl.ds(pl.multiple_of(dest * i_block, i_block), i_block)
                rows = sum(ref[block, :] for ref in visc_refs)
                rows = jnp.concatenate([rows, jnp.zeros((i_block, width - own), F32)], 1)
                fill = out_ref.shape[1] - i_part * own - i_block
                if fill:
                    rows = jnp.concatenate([rows, jnp.zeros((fill, width), F32)], 0)
                out_ref[j, i_part * own:] = rows.astype(out_ref.dtype)


def prepare(plan, masks, cells_z, idx, sources, edges, own):
    operands = list(sources) + ([] if edges is None else [edges])
    copies, interior = plan
    rows = max(at + stop - start for _, start, stop, at in copies)
    count = sum(stop - start for start, stop in interior)
    _, comps, part, width = sources[0].shape
    lanes = part * len(masks)
    tile = max(own, 16)
    batch = max(1, min(max(stop - start for start, stop in interior), 2048 // lanes))
    return pl.pallas_call(
        functools.partial(prepare_kernel, plan, masks, cells_z, tile // own),
        out_shape=(
            jax.ShapeDtypeStruct((rows, comps, lanes, width), BF16),
            jax.ShapeDtypeStruct((rows, comps, width // 8, 8, lanes), F32),
            jax.ShapeDtypeStruct((count, comps, tile, lanes), F32),
            jax.ShapeDtypeStruct((count, comps - 1, comps, tile, lanes), BF16),
            jax.ShapeDtypeStruct((width, own), F32),
        ),
        in_specs=[SMEM] + [VMEM] * len(operands),
        out_specs=(VMEM,) * 5,
        scratch_shapes=[
            pltpu.VMEM((comps, comps, width // 8, 8, lanes), F32),
            pltpu.VMEM((width, batch * comps * comps * lanes), BF16),
            pltpu.VMEM((own, batch * comps * comps * lanes), BF16),
        ],
        compiler_params=pltpu.CompilerParams(vmem_limit_bytes=vmem_limit(lanes)),
        name="prepare",
    )(idx, *operands)


def project(plans, stage, parts, idx, states, own, peers, dtype, prior=(), viscous=True, earlier=()):
    _, comps, lanes, width = states[0][0].shape
    i_block = width // peers
    i_part = i_block // PARTS
    count = 1 if stage is None else peers >> (stage + 1)
    sizes = [i_part * own + (max(16, i_block) if part == 0 and viscous else 0) for part in parts]
    depth = sum(state[3].shape[0] for state in states) * comps * lanes
    flops = 2 * len(parts) * count * i_part * own * depth * width
    layout = [(part, count, i_block, i_part) for part in parts]
    operands = [array for state in states for array in state] + list(prior)
    operands += [state[4] for state in earlier]
    return pl.pallas_call(
        functools.partial(main_kernel, plans, own, stage, layout, bool(prior), viscous, len(earlier)),
        out_shape=[jax.ShapeDtypeStruct((count, rows, width), dtype) for rows in sizes],
        in_specs=[SMEM] + [VMEM] * len(operands),
        out_specs=[VMEM] * len(parts),
        compiler_params=pltpu.CompilerParams(vmem_limit_bytes=vmem_limit(lanes)),
        cost_estimate=pl.CostEstimate(flops=4 * flops, bytes_accessed=2**20, transcendentals=0),
        name="project",
    )(idx, *operands)


def arrived(results, part, code):
    found = []
    for stage, blocks in enumerate(results):
        for j in range(blocks.shape[0]):
            if code_of(part, stage, j) ^ (1 << bit_of(part, stage)) == code:
                found.append(blocks[j].astype(F32))
    return sum(found)


def body(modes):
    cells_x, cells_y, cells_z, comps, width = modes.shape
    peers_x, peers_y = lax.axis_size("gx"), lax.axis_size("gy")
    total_points = cells_x * cells_y * cells_z * peers_x * peers_y
    own = width // peers_y
    i_block = width // peers_x
    i_part = i_block // PARTS
    idx = jnp.stack([lax.axis_index("gy"), lax.axis_index("gx")]).astype(jnp.int32)
    block = modes.transpose(0, 3, 1, 2, 4).reshape(cells_x, comps, cells_y * cells_z, width)
    up = [(i, (i + 1) % peers_x) for i in range(peers_x)]
    down = [(j, i) for i, j in up]
    quarter = cells_x // 4
    middle = block[quarter - 2:cells_x - quarter + 2]
    pieces, masks = gathered(middle, "gy")
    before = lax.ppermute(block[-2:], "gx", up)
    after = lax.ppermute(block[:2], "gx", down)
    length = middle.shape[0]
    plans = (
        (((0, 0, length, 0),), ((2, length - 2),)),
        (
            ((1, 0, quarter, 0), (0, 0, 4, quarter), (0, length - 4, length, quarter + 4),
             (1, quarter, 2 * quarter, quarter + 8)),
            ((2, quarter + 2), (quarter + 6, 2 * quarter + 6)),
        ),
    )
    stages = peers_x.bit_length() - 1
    both = tuple(range(PARTS))
    results = [[], []]
    states = [prepare(plans[0], masks, cells_z, idx, pieces, None, own)]
    rim = gathered_stack(
        jnp.concatenate([before, block[:quarter - 2], block[cells_x - quarter + 2:], after], 0),
        "gy", states[0][4],
    )
    begun = project(plans[:1], 0, both, idx, states, own, peers_x, F32, viscous=False)
    states.append(prepare(plans[1], masks, cells_z, idx, pieces, rim, own))
    sends = project(plans[1:], 0, both, idx, states[1:], own, peers_x, BF16, prior=begun, earlier=states[:1])
    for part in both:
        results[part].append(swap(sends[part], "gx", 1 << bit_of(part, 0)))
    idx, sends = lax.optimization_barrier((idx, sends))
    for stage in range(1, stages):
        kept = project(plans, stage, both, idx, states, own, peers_x, F32)
        sums = [
            jnp.stack([kept[part][j] + arrived(results[part], part, code_of(part, stage, j))
                       for j in range(kept[part].shape[0])]).astype(BF16)
            for part in both
        ]
        if bit_of(0, stage) == bit_of(1, stage):
            rows = sums[0].shape[1]
            joined = swap(jnp.concatenate(sums, 1), "gx", 1 << stage)
            got = [joined[:, :rows], joined[:, rows:]]
        else:
            got = [swap(sums[part], "gx", 1 << bit_of(part, stage)) for part in both]
        for part in both:
            results[part].append(got[part])
        idx, sums = lax.optimization_barrier((idx, sums))
    kept = project(plans, None, both, idx, states, own, peers_x, F32)
    finals = [kept[part][0] + arrived(results[part], part, 0) for part in both]
    convective = jnp.concatenate(
        [f[:i_part * own].reshape(i_part, own, width) for f in finals], 0
    ) * (-1.0 / math.sqrt(total_points))
    viscous = finals[0][i_part * own:i_part * own + i_block, :own] * (-1.0 / total_points)
    return (convective, viscous)


def solution(mesh):
    in_specs = (P("gx", "gy", None, None, None),)
    out_specs = (P("gx", "gy", None), P("gx", "gy"))
    return jax.shard_map(body, mesh=mesh, in_specs=in_specs, out_specs=out_specs, check_vma=False)
```

```python
import functools
import math

import jax
import jax.numpy as jnp
from jax import lax
from jax.experimental import pallas as pl
from jax.experimental.pallas import tpu as pltpu
from jax.sharding import PartitionSpec as P

BF16, F32 = jnp.bfloat16, jnp.float32
VMEM = pl.BlockSpec(memory_space=pltpu.VMEM)
SMEM = pl.BlockSpec(memory_space=pltpu.SMEM)
PARTS = 2
K_ROWS = 4


def group_rows(lanes):
    return 32 if lanes <= 128 else 8


def vmem_limit(lanes):
    return min(52, 16 * -(-lanes // 128)) * 2**20


def swap(x, axis, mask):
    return lax.ppermute(x, axis, [(i, i ^ mask) for i in range(lax.axis_size(axis))])


def gathered(x, axis):
    pieces, mask = [x], lax.axis_size(axis) // 2
    masks = [0]
    while mask:
        pieces += [swap(piece, axis, mask) for piece in pieces]
        masks += [m ^ mask for m in masks]
        mask //= 2
    return pieces, masks


def gathered_stack(x, axis, behind):
    stack, mask = x[None], lax.axis_size(axis) // 2
    while mask:
        got = swap(stack, axis, mask)
        if behind is not None:
            stack, got, behind = *lax.optimization_barrier((stack, got, behind))[:2], None
        stack = jnp.concatenate([stack, got], 0)
        mask //= 2
    return stack


def y_and_z_weights(lanes, cells_z):
    q = lax.broadcasted_iota(jnp.int32, (lanes, lanes), 0)
    p = lax.broadcasted_iota(jnp.int32, (lanes, lanes), 1)
    apart = q - p
    around = jnp.where(apart < 0, apart + lanes, apart)
    same = lax.div(q, cells_z) == lax.div(p, cells_z)
    weights_y = jnp.zeros((lanes, lanes), F32)
    weights_z = jnp.zeros((lanes, lanes), F32)
    for step, weight in ((1, 8.0), (-1, -8.0), (2, -1.0), (-2, 1.0)):
        weights_y = weights_y + jnp.where(around == (step * cells_z) % lanes, weight, 0.0)
        weights_z = weights_z + jnp.where(same & (apart == step), weight, 0.0)
    return jnp.concatenate([weights_y, weights_z], 1).astype(BF16)


def prepare_kernel(plan, masks, cells_z, repeat, idx_ref, *refs):
    copies, interior = plan
    pieces = len(masks)
    extra = 2 if any(source for source, *_ in copies) else 0
    sources = [refs[:pieces]]
    if extra:
        sources.append([refs[pieces].at[q] for q in range(pieces)])
    full_ref, turned_ref, first_ref, grad_ref, visc_ref, slope_ref, every_ref, mine_ref = refs[pieces + extra:]
    rows, comps, lanes, width = full_ref.shape
    part = lanes // pieces
    me = idx_ref[0]
    own = width // pieces
    for q, mask in enumerate(masks):
        slot = pl.multiple_of((me ^ mask) * part, part)
        for source, start, stop, at in copies:
            full_ref[at:at + stop - start, :, pl.ds(slot, part), :] = sources[source][q][start:stop]

    def turn(row, carry):
        for comp in range(comps):
            flat = full_ref[row, comp].astype(F32).T
            turned_ref[row, comp] = flat.reshape(width // 8, 8, lanes)
        return carry

    for source, start, stop, at in copies:
        count = stop - start
        if extra and source == 0:
            turned_ref[at:at + count] = refs[pieces + 1][start:stop]
        else:
            lax.fori_loop(at, at + count, turn, 0, unroll=count if count % 4 else 4)
    weights = y_and_z_weights(lanes, cells_z)

    def slopes(at, slot, row):
        mine, every = [], []
        for comp in range(comps):
            def line(step):
                return turned_ref[row + step, comp].reshape(width, lanes)

            along_x = (8.0 * (line(1) - line(-1)) - (line(2) - line(-2))) * (1.0 / 12.0)
            others = jnp.dot(line(0).astype(BF16), weights, preferred_element_type=F32) * (1.0 / 12.0)
            for b, value in enumerate((along_x, others[:, :lanes], others[:, lanes:])):
                slope_ref[b, comp] = value.reshape(width // 8, 8, lanes)
                every.append(value.astype(BF16))
        for b in range(comps):
            for comp in range(comps):
                block = slope_ref[b, comp, pl.ds(me * (own // 8), own // 8)].reshape(own, lanes).astype(BF16)
                mine.append((b, comp, block))
                tiled = jnp.concatenate([block] * repeat, 0)
                if b == 0:
                    first_ref[at, comp] = tiled.astype(F32)
                else:
                    grad_ref[at, b - 1, comp] = tiled
        mine = [m[2] for m in sorted(mine, key=lambda m: (m[1], m[0]))]
        column = pl.ds(pl.multiple_of(slot * (comps * comps * lanes), lanes), comps * comps * lanes)
        every_ref[:, column] = jnp.concatenate(every, 1)
        mine_ref[:, column] = jnp.concatenate(mine, 1)

    batch = mine_ref.shape[1] // (comps * comps * lanes)
    steps = [(row, min(row + batch, stop)) for start, stop in interior for row in range(start, stop, batch)]
    at = 0
    for start, stop in steps:
        def one(step, carry, start=start, at=at):
            slopes(at + step, step, start + step)
            return carry

        lax.fori_loop(0, stop - start, one, 0, unroll=5 if (stop - start) % 5 == 0 else min(4, stop - start))
        used = (stop - start) * comps * comps * lanes
        term = lax.dot_general(
            every_ref[:, :used], mine_ref[:, :used], (((1,), (1,)), ((), ())), preferred_element_type=F32
        )
        visc_ref[...] = term if at == 0 else visc_ref[...] + term
        at += stop - start


def code_of(part, stage, j):
    if part == 0 or stage >= 2:
        return (2 * j + 1) << stage
    if stage == 0:
        return (j & 1) | 2 | ((j >> 1) << 2)
    return 1 | (j << 2)


def bit_of(part, stage):
    return 1 - stage if part == 1 and stage < 2 else stage


def main_kernel(plans, own, stage, parts, prior, viscous, earlier, idx_ref, *refs):
    states = [refs[5 * n:5 * n + 5] for n in range(len(plans))]
    prior_refs = refs[5 * len(plans):5 * len(plans) + (len(parts) if prior else 0)]
    out_refs = refs[len(refs) - len(parts):]
    visc_refs = [state[4] for state in states] + list(refs[len(refs) - len(parts) - earlier:len(refs) - len(parts)])
    rows_of = [[r for start, stop in plan[1] for r in range(start, stop)] for plan in plans]
    _, comps, lanes, width = states[0][0].shape
    i_block, i_part = parts[0][2], parts[0][3]
    tile = states[0][3].shape[3]
    joint = tile // own
    me = idx_ref[1]
    depth = comps * lanes

    def code(part, j):
        return 0 if stage is None else code_of(part, stage, j)

    def group(jobs):
        def source(i):
            part, j = jobs[i // i_part]
            row = (me ^ code(part, j)) * i_block + part * i_part
            if i_part % 8 == 0:
                return row // 8 + (i % i_part) // 8, i % 8
            return row // 8, (part * i_part) % 8 + i % i_part

        def pairs(state, interior, x, i):
            _, turned_ref, first_ref, grad_ref, _ = state
            pieces = []
            for lane in range(0, lanes, 128):
                cut = slice(lane, lane + 128)
                wide, narrow = [], []
                for a in range(comps):
                    lines = []
                    for j in range(joint):
                        lead, sub = source(i + j)
                        line = turned_ref[interior[x], a, lead, sub:sub + 1, cut]
                        lines.append(jnp.broadcast_to(line, (own, 128)))
                    wide.append(jnp.concatenate(lines, 0))
                    half = wide[-1][:16].astype(BF16)
                    narrow.append(jnp.concatenate([half] * (tile // 16), 0))
                row = []
                for b in range(comps):
                    phis = wide if b == 0 else narrow
                    slope = [first_ref[x, a, :, cut] if b == 0 else grad_ref[x, b - 1, a, :, cut]
                             for a in range(comps)]
                    pair = phis[0] * slope[0]
                    for a in range(1, comps):
                        pair = pair + phis[a] * slope[a]
                    row.append(pair.astype(BF16))
                pieces.append(row)
            return [pieces[l][b] for b in range(comps) for l in range(lanes // 128)]

        total = None
        for state, interior in zip(states, rows_of):
            k_rows = K_ROWS if len(interior) % K_ROWS == 0 else 6
            for first in range(0, len(interior), k_rows):
                count = min(k_rows, len(interior) - first)
                left = jnp.concatenate([
                    jnp.concatenate(
                        [p for x in range(first, first + count) for p in pairs(state, interior, x, i)], 1
                    )
                    for i in range(0, len(jobs) * i_part, joint)
                ], 0)
                right = jnp.concatenate(
                    [state[0][row].reshape(depth, width) for row in interior[first:first + count]], 0
                )
                term = jnp.dot(left, right, preferred_element_type=F32)
                total = term if total is None else total + term
        return total.reshape(len(jobs), i_part * own, width)

    jobs = [(part, j) for part, count, _, _ in parts for j in range(count)]
    at_once = group_rows(lanes) // i_part

    def put(n, low, value):
        if prior:
            value = value + prior_refs[n][pl.ds(low, value.shape[0])]
        out_refs[n][pl.ds(low, value.shape[0]), :i_part * own] = value.astype(out_refs[n].dtype)

    if len(jobs) <= at_once:
        value, at = group(jobs), 0
        for n, (_, count, _, _) in enumerate(parts):
            put(n, 0, value[at:at + count])
            at += count
    else:
        for n, (part, count, _, _) in enumerate(parts):
            size = min(at_once, count)

            def one(step, carry, n=n, part=part, size=size):
                low = step * size
                put(n, low, group([(part, low + j) for j in range(size)]))
                return carry

            lax.fori_loop(0, count // size, one, 0)
    for (part, count, _, _), out_ref in zip(parts, out_refs):
        if part == 0 and viscous:
            for j in range(count):
                dest = me ^ code(part, j)
                block = pl.ds(pl.multiple_of(dest * i_block, i_block), i_block)
                rows = sum(ref[block, :] for ref in visc_refs)
                rows = jnp.concatenate([rows, jnp.zeros((i_block, width - own), F32)], 1)
                fill = out_ref.shape[1] - i_part * own - i_block
                if fill:
                    rows = jnp.concatenate([rows, jnp.zeros((fill, width), F32)], 0)
                out_ref[j, i_part * own:] = rows.astype(out_ref.dtype)


def prepare(plan, masks, cells_z, idx, sources, extra, own):
    operands = list(sources) + list(extra)
    copies, interior = plan
    rows = max(at + stop - start for _, start, stop, at in copies)
    count = sum(stop - start for start, stop in interior)
    _, comps, part, width = sources[0].shape
    lanes = part * len(masks)
    tile = max(own, 16)
    batch = max(1, min(max(stop - start for start, stop in interior), 2048 // lanes))
    return pl.pallas_call(
        functools.partial(prepare_kernel, plan, masks, cells_z, tile // own),
        out_shape=(
            jax.ShapeDtypeStruct((rows, comps, lanes, width), BF16),
            jax.ShapeDtypeStruct((rows, comps, width // 8, 8, lanes), F32),
            jax.ShapeDtypeStruct((count, comps, tile, lanes), F32),
            jax.ShapeDtypeStruct((count, comps - 1, comps, tile, lanes), BF16),
            jax.ShapeDtypeStruct((width, own), F32),
        ),
        in_specs=[SMEM] + [VMEM] * len(operands),
        out_specs=(VMEM,) * 5,
        scratch_shapes=[
            pltpu.VMEM((comps, comps, width // 8, 8, lanes), F32),
            pltpu.VMEM((width, batch * comps * comps * lanes), BF16),
            pltpu.VMEM((own, batch * comps * comps * lanes), BF16),
        ],
        compiler_params=pltpu.CompilerParams(vmem_limit_bytes=vmem_limit(lanes)),
        name="prepare",
    )(idx, *operands)


def project(plans, stage, parts, idx, states, own, peers, dtype, prior=(), viscous=True, earlier=()):
    _, comps, lanes, width = states[0][0].shape
    i_block = width // peers
    i_part = i_block // PARTS
    count = 1 if stage is None else peers >> (stage + 1)
    sizes = [i_part * own + (max(16, i_block) if part == 0 and viscous else 0) for part in parts]
    depth = sum(state[3].shape[0] for state in states) * comps * lanes
    flops = 2 * len(parts) * count * i_part * own * depth * width
    layout = [(part, count, i_block, i_part) for part in parts]
    operands = [array for state in states for array in state] + list(prior)
    operands += [state[4] for state in earlier]
    return pl.pallas_call(
        functools.partial(main_kernel, plans, own, stage, layout, bool(prior), viscous, len(earlier)),
        out_shape=[jax.ShapeDtypeStruct((count, rows, width), dtype) for rows in sizes],
        in_specs=[SMEM] + [VMEM] * len(operands),
        out_specs=[VMEM] * len(parts),
        compiler_params=pltpu.CompilerParams(vmem_limit_bytes=vmem_limit(lanes)),
        cost_estimate=pl.CostEstimate(flops=4 * flops, bytes_accessed=2**20, transcendentals=0),
        name="project",
    )(idx, *operands)


def arrived(results, part, code):
    found = []
    for stage, blocks in enumerate(results):
        for j in range(blocks.shape[0]):
            if code_of(part, stage, j) ^ (1 << bit_of(part, stage)) == code:
                found.append(blocks[j].astype(F32))
    return sum(found)


def finish_kernel(scales, parts, *refs):
    convective_ref, viscous_ref = refs[-2:]
    i_block, own, width = convective_ref.shape
    i_part = i_block // parts
    each = (len(refs) - 2) // parts
    for part in range(parts):
        total = refs[part * each][0]
        for ref in refs[part * each + 1:(part + 1) * each]:
            total = total + ref[0].astype(F32)
        rows = total[:i_part * own] * scales[0]
        convective_ref[part * i_part:(part + 1) * i_part] = rows.reshape(i_part, own, width)
        if part == 0:
            viscous_ref[...] = total[i_part * own:i_part * own + i_block, :own] * scales[1]


def body(modes):
    cells_x, cells_y, cells_z, comps, width = modes.shape
    peers_x, peers_y = lax.axis_size("gx"), lax.axis_size("gy")
    total_points = cells_x * cells_y * cells_z * peers_x * peers_y
    own = width // peers_y
    i_block = width // peers_x
    i_part = i_block // PARTS
    idx = jnp.stack([lax.axis_index("gy"), lax.axis_index("gx")]).astype(jnp.int32)
    block = modes.transpose(0, 3, 1, 2, 4).reshape(cells_x, comps, cells_y * cells_z, width)
    up = [(i, (i + 1) % peers_x) for i in range(peers_x)]
    down = [(j, i) for i, j in up]
    quarter = max(2, cells_x // 5)
    middle = block[quarter - 2:cells_x - quarter + 2]
    pieces, masks = gathered(middle, "gy")
    before = lax.ppermute(block[-2:], "gx", up)
    after = lax.ppermute(block[:2], "gx", down)
    length = middle.shape[0]
    plans = (
        (((0, 0, length, 0),), ((2, length - 2),)),
        (
            ((1, 0, quarter, 0), (0, 0, 4, quarter), (0, length - 4, length, quarter + 4),
             (1, quarter, 2 * quarter, quarter + 8)),
            ((2, quarter + 2), (quarter + 6, 2 * quarter + 6)),
        ),
    )
    stages = peers_x.bit_length() - 1
    both = tuple(range(PARTS))
    results = [[], []]
    states = [prepare(plans[0], masks, cells_z, idx, pieces, (), own)]
    rim = gathered_stack(
        jnp.concatenate([before, block[:quarter - 2], block[cells_x - quarter + 2:], after], 0),
        "gy", states[0][4],
    )
    begun = project(plans[:1], 0, both, idx, states, own, peers_x, F32, viscous=False)
    states.append(prepare(plans[1], masks, cells_z, idx, pieces, (rim, states[0][1]), own))
    sends = project(plans[1:], 0, both, idx, states[1:], own, peers_x, BF16, prior=begun, earlier=states[:1])
    for part in both:
        results[part].append(swap(sends[part], "gx", 1 << bit_of(part, 0)))
    idx, sends = lax.optimization_barrier((idx, sends))
    for stage in range(1, stages):
        kept = project(plans, stage, both, idx, states, own, peers_x, F32)
        sums = [
            jnp.stack([kept[part][j] + arrived(results[part], part, code_of(part, stage, j))
                       for j in range(kept[part].shape[0])]).astype(BF16)
            for part in both
        ]
        if bit_of(0, stage) == bit_of(1, stage):
            rows = sums[0].shape[1]
            joined = swap(jnp.concatenate(sums, 1), "gx", 1 << stage)
            got = [joined[:, :rows], joined[:, rows:]]
        else:
            got = [swap(sums[part], "gx", 1 << bit_of(part, stage)) for part in both]
        for part in both:
            results[part].append(got[part])
        idx, sums = lax.optimization_barrier((idx, sums))
    kept = project(plans, None, both, idx, states, own, peers_x, F32)
    scales = (-1.0 / math.sqrt(total_points), -1.0 / total_points)
    blocks = [blocks for part in both for blocks in (kept[part], *results[part])]
    convective, viscous = pl.pallas_call(
        functools.partial(finish_kernel, scales, len(both)),
        out_shape=(
            jax.ShapeDtypeStruct((i_block, own, width), F32),
            jax.ShapeDtypeStruct((i_block, own), F32),
        ),
        in_specs=[VMEM] * len(blocks),
        out_specs=(VMEM,) * 2,
        name="finish",
    )(*blocks)
    return (convective, viscous)


def solution(mesh):
    in_specs = (P("gx", "gy", None, None, None),)
    out_specs = (P("gx", "gy", None), P("gx", "gy"))
    return jax.shard_map(body, mesh=mesh, in_specs=in_specs, out_specs=out_specs, check_vma=False)
```

```python
import functools
import math

import jax
import jax.numpy as jnp
from jax import lax
from jax.experimental import pallas as pl
from jax.experimental.pallas import tpu as pltpu
from jax.sharding import PartitionSpec as P

BF16, F32 = jnp.bfloat16, jnp.float32
VMEM = pl.BlockSpec(memory_space=pltpu.VMEM)
SMEM = pl.BlockSpec(memory_space=pltpu.SMEM)
PARTS = 2
K_ROWS = 4


def group_rows(lanes):
    return 32 if lanes <= 128 else 8


def vmem_limit(lanes):
    return min(52, 16 * -(-lanes // 128)) * 2**20


def swap(x, axis, mask):
    return lax.ppermute(x, axis, [(i, i ^ mask) for i in range(lax.axis_size(axis))])


def gathered(x, axis):
    pieces, mask = [x], lax.axis_size(axis) // 2
    masks = [0]
    while mask:
        pieces += [swap(piece, axis, mask) for piece in pieces]
        masks += [m ^ mask for m in masks]
        mask //= 2
    return pieces, masks


def gathered_stack(x, axis, behind):
    stack, mask = x[None], lax.axis_size(axis) // 2
    while mask:
        got = swap(stack, axis, mask)
        if behind is not None:
            stack, got, behind = *lax.optimization_barrier((stack, got, behind))[:2], None
        stack = jnp.concatenate([stack, got], 0)
        mask //= 2
    return stack


def y_and_z_weights(lanes, cells_z):
    q = lax.broadcasted_iota(jnp.int32, (lanes, lanes), 0)
    p = lax.broadcasted_iota(jnp.int32, (lanes, lanes), 1)
    apart = q - p
    around = jnp.where(apart < 0, apart + lanes, apart)
    same = lax.div(q, cells_z) == lax.div(p, cells_z)
    weights_y = jnp.zeros((lanes, lanes), F32)
    weights_z = jnp.zeros((lanes, lanes), F32)
    for step, weight in ((1, 8.0), (-1, -8.0), (2, -1.0), (-2, 1.0)):
        weights_y = weights_y + jnp.where(around == (step * cells_z) % lanes, weight, 0.0)
        weights_z = weights_z + jnp.where(same & (apart == step), weight, 0.0)
    return jnp.concatenate([weights_y, weights_z], 1).astype(BF16)


def prepare_kernel(plan, masks, cells_z, repeat, idx_ref, *refs):
    copies, interior = plan
    pieces = len(masks)
    extra = 2 if any(source for source, *_ in copies) else 0
    sources = [refs[:pieces]]
    if extra:
        sources.append([refs[pieces].at[q] for q in range(pieces)])
    full_ref, turned_ref, first_ref, grad_ref, visc_ref, every_ref, mine_ref = refs[pieces + extra:]
    rows, comps, lanes, width = full_ref.shape
    part = lanes // pieces
    me = idx_ref[0]
    own = width // pieces
    for q, mask in enumerate(masks):
        slot = pl.multiple_of((me ^ mask) * part, part)
        for source, start, stop, at in copies:
            full_ref[at:at + stop - start, :, pl.ds(slot, part), :] = sources[source][q][start:stop]

    def turn(row, carry):
        for comp in range(comps):
            flat = full_ref[row, comp].astype(F32).T
            turned_ref[row, comp] = flat.reshape(width // 8, 8, lanes)
        return carry

    for source, start, stop, at in copies:
        count = stop - start
        if extra and source == 0:
            turned_ref[at:at + count] = refs[pieces + 1][start:stop]
        else:
            lax.fori_loop(at, at + count, turn, 0, unroll=count if count % 4 else 4)
    weights = y_and_z_weights(lanes, cells_z)

    def derivatives(line):
        along_x = (8.0 * (line(1) - line(-1)) - (line(2) - line(-2))) * (1.0 / 12.0)
        others = jnp.dot(line(0).astype(BF16), weights, preferred_element_type=F32) * (1.0 / 12.0)
        return [value.astype(BF16) for value in (along_x, others[:, :lanes], others[:, lanes:])]

    def slopes(at, slot, row):
        mine, every = [], []
        for comp in range(comps):
            def all_rows(step):
                return turned_ref[row + step, comp].reshape(width, lanes)

            def own_rows(step):
                return turned_ref[row + step, comp, pl.ds(me * (own // 8), own // 8)].reshape(own, lanes)

            every += derivatives(all_rows)
            for b, block in enumerate(derivatives(own_rows)):
                mine.append(block)
                tiled = jnp.concatenate([block] * repeat, 0)
                if b == 0:
                    first_ref[at, comp] = tiled.astype(F32)
                else:
                    grad_ref[at, b - 1, comp] = tiled
        column = pl.ds(pl.multiple_of(slot * (comps * comps * lanes), lanes), comps * comps * lanes)
        every_ref[:, column] = jnp.concatenate(every, 1)
        mine_ref[:, column] = jnp.concatenate(mine, 1)

    batch = mine_ref.shape[1] // (comps * comps * lanes)
    steps = [(row, min(row + batch, stop)) for start, stop in interior for row in range(start, stop, batch)]
    at = 0
    for start, stop in steps:
        def one(step, carry, start=start, at=at):
            slopes(at + step, step, start + step)
            return carry

        lax.fori_loop(0, stop - start, one, 0, unroll=5 if (stop - start) % 5 == 0 else min(4, stop - start))
        used = (stop - start) * comps * comps * lanes
        term = lax.dot_general(
            every_ref[:, :used], mine_ref[:, :used], (((1,), (1,)), ((), ())), preferred_element_type=F32
        )
        visc_ref[...] = term if at == 0 else visc_ref[...] + term
        at += stop - start


def code_of(part, stage, j):
    if part == 0 or stage >= 2:
        return (2 * j + 1) << stage
    if stage == 0:
        return (j & 1) | 2 | ((j >> 1) << 2)
    return 1 | (j << 2)


def bit_of(part, stage):
    return 1 - stage if part == 1 and stage < 2 else stage


def main_kernel(plans, own, stage, parts, prior, viscous, earlier, idx_ref, *refs):
    states = [refs[5 * n:5 * n + 5] for n in range(len(plans))]
    prior_refs = refs[5 * len(plans):5 * len(plans) + (len(parts) if prior else 0)]
    out_refs = refs[len(refs) - len(parts):]
    visc_refs = [state[4] for state in states] + list(refs[len(refs) - len(parts) - earlier:len(refs) - len(parts)])
    rows_of = [[r for start, stop in plan[1] for r in range(start, stop)] for plan in plans]
    _, comps, lanes, width = states[0][0].shape
    i_block, i_part = parts[0][2], parts[0][3]
    tile = states[0][3].shape[3]
    joint = tile // own
    me = idx_ref[1]
    depth = comps * lanes

    def code(part, j):
        return 0 if stage is None else code_of(part, stage, j)

    def group(jobs):
        def source(i):
            part, j = jobs[i // i_part]
            row = (me ^ code(part, j)) * i_block + part * i_part
            if i_part % 8 == 0:
                return row // 8 + (i % i_part) // 8, i % 8
            return row // 8, (part * i_part) % 8 + i % i_part

        def pairs(state, interior, x, i):
            _, turned_ref, first_ref, grad_ref, _ = state
            pieces = []
            for lane in range(0, lanes, 128):
                cut = slice(lane, lane + 128)
                wide, narrow = [], []
                for a in range(comps):
                    lines = []
                    for j in range(joint):
                        lead, sub = source(i + j)
                        line = turned_ref[interior[x], a, lead, sub:sub + 1, cut]
                        lines.append(jnp.broadcast_to(line, (own, 128)))
                    wide.append(jnp.concatenate(lines, 0))
                    half = wide[-1][:16].astype(BF16)
                    narrow.append(jnp.concatenate([half] * (tile // 16), 0))
                row = []
                for b in range(comps):
                    phis = wide if b == 0 else narrow
                    slope = [first_ref[x, a, :, cut] if b == 0 else grad_ref[x, b - 1, a, :, cut]
                             for a in range(comps)]
                    pair = phis[0] * slope[0]
                    for a in range(1, comps):
                        pair = pair + phis[a] * slope[a]
                    row.append(pair.astype(BF16))
                pieces.append(row)
            return [pieces[l][b] for b in range(comps) for l in range(lanes // 128)]

        total = None
        for state, interior in zip(states, rows_of):
            k_rows = K_ROWS if len(interior) % K_ROWS == 0 else 6
            for first in range(0, len(interior), k_rows):
                count = min(k_rows, len(interior) - first)
                left = jnp.concatenate([
                    jnp.concatenate(
                        [p for x in range(first, first + count) for p in pairs(state, interior, x, i)], 1
                    )
                    for i in range(0, len(jobs) * i_part, joint)
                ], 0)
                right = jnp.concatenate(
                    [state[0][row].reshape(depth, width) for row in interior[first:first + count]], 0
                )
                term = jnp.dot(left, right, preferred_element_type=F32)
                total = term if total is None else total + term
        return total.reshape(len(jobs), i_part * own, width)

    jobs = [(part, j) for part, count, _, _ in parts for j in range(count)]
    at_once = group_rows(lanes) // i_part

    def put(n, low, value):
        if prior:
            value = value + prior_refs[n][pl.ds(low, value.shape[0])]
        out_refs[n][pl.ds(low, value.shape[0]), :i_part * own] = value.astype(out_refs[n].dtype)

    if len(jobs) <= at_once:
        value, at = group(jobs), 0
        for n, (_, count, _, _) in enumerate(parts):
            put(n, 0, value[at:at + count])
            at += count
    else:
        for n, (part, count, _, _) in enumerate(parts):
            size = min(at_once, count)

            def one(step, carry, n=n, part=part, size=size):
                low = step * size
                put(n, low, group([(part, low + j) for j in range(size)]))
                return carry

            lax.fori_loop(0, count // size, one, 0)
    for (part, count, _, _), out_ref in zip(parts, out_refs):
        if part == 0 and viscous:
            for j in range(count):
                dest = me ^ code(part, j)
                block = pl.ds(pl.multiple_of(dest * i_block, i_block), i_block)
                rows = sum(ref[block, :] for ref in visc_refs)
                rows = jnp.concatenate([rows, jnp.zeros((i_block, width - own), F32)], 1)
                fill = out_ref.shape[1] - i_part * own - i_block
                if fill:
                    rows = jnp.concatenate([rows, jnp.zeros((fill, width), F32)], 0)
                out_ref[j, i_part * own:] = rows.astype(out_ref.dtype)


def prepare(plan, masks, cells_z, idx, sources, extra, own):
    operands = list(sources) + list(extra)
    copies, interior = plan
    rows = max(at + stop - start for _, start, stop, at in copies)
    count = sum(stop - start for start, stop in interior)
    _, comps, part, width = sources[0].shape
    lanes = part * len(masks)
    tile = max(own, 16)
    batch = max(1, min(max(stop - start for start, stop in interior), 2048 // lanes))
    return pl.pallas_call(
        functools.partial(prepare_kernel, plan, masks, cells_z, tile // own),
        out_shape=(
            jax.ShapeDtypeStruct((rows, comps, lanes, width), BF16),
            jax.ShapeDtypeStruct((rows, comps, width // 8, 8, lanes), F32),
            jax.ShapeDtypeStruct((count, comps, tile, lanes), F32),
            jax.ShapeDtypeStruct((count, comps - 1, comps, tile, lanes), BF16),
            jax.ShapeDtypeStruct((width, own), F32),
        ),
        in_specs=[SMEM] + [VMEM] * len(operands),
        out_specs=(VMEM,) * 5,
        scratch_shapes=[
            pltpu.VMEM((width, batch * comps * comps * lanes), BF16),
            pltpu.VMEM((own, batch * comps * comps * lanes), BF16),
        ],
        compiler_params=pltpu.CompilerParams(vmem_limit_bytes=vmem_limit(lanes)),
        name="prepare",
    )(idx, *operands)


def project(plans, stage, parts, idx, states, own, peers, dtype, prior=(), viscous=True, earlier=()):
    _, comps, lanes, width = states[0][0].shape
    i_block = width // peers
    i_part = i_block // PARTS
    count = 1 if stage is None else peers >> (stage + 1)
    sizes = [i_part * own + (max(16, i_block) if part == 0 and viscous else 0) for part in parts]
    depth = sum(state[3].shape[0] for state in states) * comps * lanes
    flops = 2 * len(parts) * count * i_part * own * depth * width
    layout = [(part, count, i_block, i_part) for part in parts]
    operands = [array for state in states for array in state] + list(prior)
    operands += [state[4] for state in earlier]
    return pl.pallas_call(
        functools.partial(main_kernel, plans, own, stage, layout, bool(prior), viscous, len(earlier)),
        out_shape=[jax.ShapeDtypeStruct((count, rows, width), dtype) for rows in sizes],
        in_specs=[SMEM] + [VMEM] * len(operands),
        out_specs=[VMEM] * len(parts),
        compiler_params=pltpu.CompilerParams(vmem_limit_bytes=vmem_limit(lanes)),
        cost_estimate=pl.CostEstimate(flops=4 * flops, bytes_accessed=2**20, transcendentals=0),
        name="project",
    )(idx, *operands)


def arrived(results, part, code):
    found = []
    for stage, blocks in enumerate(results):
        for j in range(blocks.shape[0]):
            if code_of(part, stage, j) ^ (1 << bit_of(part, stage)) == code:
                found.append(blocks[j].astype(F32))
    return sum(found)


def finish_kernel(scales, terms, *refs):
    convective_ref, viscous_ref = refs[-2:]
    i_block, own, width = convective_ref.shape
    i_part = i_block // len(terms)
    for part, found in enumerate(terms):
        total = sum(refs[n][0, start:stop].astype(F32) for n, start, stop in found)
        rows = total[:i_part * own] * scales[0]
        convective_ref[part * i_part:(part + 1) * i_part] = rows.reshape(i_part, own, width)
        if part == 0:
            viscous_ref[...] = total[i_part * own:i_part * own + i_block, :own] * scales[1]


def body(modes):
    cells_x, cells_y, cells_z, comps, width = modes.shape
    peers_x, peers_y = lax.axis_size("gx"), lax.axis_size("gy")
    total_points = cells_x * cells_y * cells_z * peers_x * peers_y
    own = width // peers_y
    i_block = width // peers_x
    i_part = i_block // PARTS
    idx = jnp.stack([lax.axis_index("gy"), lax.axis_index("gx")]).astype(jnp.int32)
    block = modes.transpose(0, 3, 1, 2, 4).reshape(cells_x, comps, cells_y * cells_z, width)
    up = [(i, (i + 1) % peers_x) for i in range(peers_x)]
    down = [(j, i) for i, j in up]
    quarter = max(2, cells_x // 5)
    middle = block[quarter - 2:cells_x - quarter + 2]
    pieces, masks = gathered(middle, "gy")
    before = lax.ppermute(block[-2:], "gx", up)
    after = lax.ppermute(block[:2], "gx", down)
    length = middle.shape[0]
    plans = (
        (((0, 0, length, 0),), ((2, length - 2),)),
        (
            ((1, 0, quarter, 0), (0, 0, 4, quarter), (0, length - 4, length, quarter + 4),
             (1, quarter, 2 * quarter, quarter + 8)),
            ((2, quarter + 2), (quarter + 6, 2 * quarter + 6)),
        ),
    )
    stages = peers_x.bit_length() - 1
    both = tuple(range(PARTS))
    results = [[], []]
    states = [prepare(plans[0], masks, cells_z, idx, pieces, (), own)]
    rim = gathered_stack(
        jnp.concatenate([before, block[:quarter - 2], block[cells_x - quarter + 2:], after], 0),
        "gy", states[0][4],
    )
    begun = project(plans[:1], 0, both, idx, states, own, peers_x, F32, viscous=False)
    states.append(prepare(plans[1], masks, cells_z, idx, pieces, (rim, states[0][1]), own))
    sends = project(plans[1:], 0, both, idx, states[1:], own, peers_x, BF16, prior=begun, earlier=states[:1])
    for part in both:
        results[part].append(swap(sends[part], "gx", 1 << bit_of(part, 0)))
    idx, sends = lax.optimization_barrier((idx, sends))
    for stage in range(1, stages):
        kept = project(plans, stage, both, idx, states, own, peers_x, F32)
        sums = [
            jnp.stack([kept[part][j] + arrived(results[part], part, code_of(part, stage, j))
                       for j in range(kept[part].shape[0])]).astype(BF16)
            for part in both
        ]
        if bit_of(0, stage) == bit_of(1, stage):
            rows = sums[0].shape[1]
            joined = swap(jnp.concatenate(sums, 1), "gx", 1 << stage)
            got = [joined[:, :rows], joined[:, rows:]]
        else:
            got = [swap(sums[part], "gx", 1 << bit_of(part, stage)) for part in both]
        for part in both:
            results[part].append(got[part])
        idx, sums = lax.optimization_barrier((idx, sums))
    kept = project(plans, None, both, idx, states, own, peers_x, F32)
    scales = (-1.0 / math.sqrt(total_points), -1.0 / total_points)
    blocks, terms = [], []
    for part in both:
        rows = kept[part].shape[1]
        blocks += [kept[part]] + results[part][:-1]
        terms.append([(n, 0, rows) for n in range(len(blocks) - stages, len(blocks))])
        terms[part].append((stages * len(both), sum(k.shape[1] for k in kept[:part]), sum(k.shape[1] for k in kept[:part + 1])))
    convective, viscous = pl.pallas_call(
        functools.partial(finish_kernel, scales, terms),
        out_shape=(
            jax.ShapeDtypeStruct((i_block, own, width), F32),
            jax.ShapeDtypeStruct((i_block, own), F32),
        ),
        in_specs=[VMEM] * (len(blocks) + 1),
        out_specs=(VMEM,) * 2,
        compiler_params=pltpu.CompilerParams(vmem_limit_bytes=4 * 2**20),
        name="finish",
    )(*blocks, joined)
    return (convective, viscous)


def solution(mesh):
    in_specs = (P("gx", "gy", None, None, None),)
    out_specs = (P("gx", "gy", None), P("gx", "gy"))
    return jax.shard_map(body, mesh=mesh, in_specs=in_specs, out_specs=out_specs, check_vma=False)
```

```python
import functools
import math

import jax
import jax.numpy as jnp
from jax import lax
from jax.experimental import pallas as pl
from jax.experimental.pallas import tpu as pltpu
from jax.sharding import PartitionSpec as P

BF16, F32 = jnp.bfloat16, jnp.float32
VMEM = pl.BlockSpec(memory_space=pltpu.VMEM)
SMEM = pl.BlockSpec(memory_space=pltpu.SMEM)
PARTS = 2
K_ROWS = 4


def group_rows(lanes):
    return 32 if lanes <= 128 else 8


def vmem_limit(lanes):
    return min(52, 16 * -(-lanes // 128)) * 2**20


def swap(x, axis, mask):
    return lax.ppermute(x, axis, [(i, i ^ mask) for i in range(lax.axis_size(axis))])


def gathered(x, axis, beside):
    pieces, masks, mask = [x], [0], lax.axis_size(axis) // 2
    first = True
    while mask:
        got = [swap(piece, axis, mask) for piece in pieces]
        if first:
            got, beside = lax.optimization_barrier((got, beside))
            first = False
        pieces += got
        masks += [m ^ mask for m in masks]
        mask //= 2
    return pieces, masks, beside


def gathered_stack(x, axis, behind):
    stack, mask = x[None], lax.axis_size(axis) // 2
    while mask:
        got = swap(stack, axis, mask)
        if behind is not None:
            stack, got, behind = *lax.optimization_barrier((stack, got, behind))[:2], None
        stack = jnp.concatenate([stack, got], 0)
        mask //= 2
    return stack


def y_and_z_weights(lanes, cells_z):
    q = lax.broadcasted_iota(jnp.int32, (lanes, lanes), 0)
    p = lax.broadcasted_iota(jnp.int32, (lanes, lanes), 1)
    apart = q - p
    around = jnp.where(apart < 0, apart + lanes, apart)
    same = lax.div(q, cells_z) == lax.div(p, cells_z)
    weights_y = jnp.zeros((lanes, lanes), F32)
    weights_z = jnp.zeros((lanes, lanes), F32)
    for step, weight in ((1, 8.0), (-1, -8.0), (2, -1.0), (-2, 1.0)):
        weights_y = weights_y + jnp.where(around == (step * cells_z) % lanes, weight, 0.0)
        weights_z = weights_z + jnp.where(same & (apart == step), weight, 0.0)
    return jnp.concatenate([weights_y, weights_z], 1).astype(BF16)


def prepare_kernel(plan, masks, cells_z, repeat, idx_ref, *refs):
    copies, interior = plan
    pieces = len(masks)
    extra = 2 if any(source for source, *_ in copies) else 0
    sources = [refs[:pieces]]
    if extra:
        sources.append([refs[pieces].at[q] for q in range(pieces)])
    full_ref, turned_ref, first_ref, grad_ref, visc_ref, every_ref, mine_ref = refs[pieces + extra:]
    rows, comps, lanes, width = full_ref.shape
    part = lanes // pieces
    me = idx_ref[0]
    own = width // pieces
    for q, mask in enumerate(masks):
        slot = pl.multiple_of((me ^ mask) * part, part)
        for source, start, stop, at in copies:
            full_ref[at:at + stop - start, :, pl.ds(slot, part), :] = sources[source][q][start:stop]

    def turn(row, carry):
        for comp in range(comps):
            flat = full_ref[row, comp].astype(F32).T
            turned_ref[row, comp] = flat.reshape(width // 8, 8, lanes)
        return carry

    for source, start, stop, at in copies:
        count = stop - start
        if extra and source == 0:
            turned_ref[at:at + count] = refs[pieces + 1][start:stop]
        else:
            lax.fori_loop(at, at + count, turn, 0, unroll=count if count % 4 else 4)
    weights = y_and_z_weights(lanes, cells_z)

    def derivatives(line):
        along_x = (8.0 * (line(1) - line(-1)) - (line(2) - line(-2))) * (1.0 / 12.0)
        others = jnp.dot(line(0).astype(BF16), weights, preferred_element_type=F32) * (1.0 / 12.0)
        return [value.astype(BF16) for value in (along_x, others[:, :lanes], others[:, lanes:])]

    def slopes(at, slot, row):
        mine, every = [], []
        for comp in range(comps):
            def all_rows(step):
                return turned_ref[row + step, comp].reshape(width, lanes)

            def own_rows(step):
                return turned_ref[row + step, comp, pl.ds(me * (own // 8), own // 8)].reshape(own, lanes)

            every += derivatives(all_rows)
            for b, block in enumerate(derivatives(own_rows)):
                mine.append(block)
                tiled = jnp.concatenate([block] * repeat, 0)
                if b == 0:
                    first_ref[at, comp] = tiled.astype(F32)
                else:
                    grad_ref[at, b - 1, comp] = tiled
        column = slot * (comps * comps * lanes)
        if not isinstance(slot, int):
            column = pl.multiple_of(column, lanes)
        column = pl.ds(column, comps * comps * lanes)
        every_ref[:, column] = jnp.concatenate(every, 1)
        mine_ref[:, column] = jnp.concatenate(mine, 1)

    batch = mine_ref.shape[1] // (comps * comps * lanes)
    if lanes <= 128:
        steps = [[row for start, stop in interior for row in range(start, stop)]]
    else:
        steps = [list(range(row, min(row + batch, stop))) for start, stop in interior for row in range(start, stop, batch)]
    at = 0
    for rows_now in steps:
        if lanes <= 128:
            for slot, row in enumerate(rows_now):
                slopes(at + slot, slot, row)
        else:
            def one(step, carry, start=rows_now[0], at=at):
                slopes(at + step, step, start + step)
                return carry

            lax.fori_loop(0, len(rows_now), one, 0)
        used = len(rows_now) * comps * comps * lanes
        term = lax.dot_general(
            every_ref[:, :used], mine_ref[:, :used], (((1,), (1,)), ((), ())), preferred_element_type=F32
        )
        visc_ref[...] = term if at == 0 else visc_ref[...] + term
        at += len(rows_now)


def code_of(part, stage, j):
    if part == 0 or stage >= 2:
        return (2 * j + 1) << stage
    if stage == 0:
        return (j & 1) | 2 | ((j >> 1) << 2)
    return 1 | (j << 2)


def bit_of(part, stage):
    return 1 - stage if part == 1 and stage < 2 else stage


def main_kernel(plans, own, stage, parts, prior, viscous, earlier, idx_ref, *refs):
    states = [refs[5 * n:5 * n + 5] for n in range(len(plans))]
    prior_refs = refs[5 * len(plans):5 * len(plans) + (len(parts) if prior else 0)]
    out_refs = refs[len(refs) - len(parts):]
    visc_refs = [state[4] for state in states] + list(refs[len(refs) - len(parts) - earlier:len(refs) - len(parts)])
    rows_of = [[r for start, stop in plan[1] for r in range(start, stop)] for plan in plans]
    _, comps, lanes, width = states[0][0].shape
    i_block, i_part = parts[0][2], parts[0][3]
    tile = states[0][3].shape[3]
    joint = tile // own
    me = idx_ref[1]
    depth = comps * lanes

    def code(part, j):
        return 0 if stage is None else code_of(part, stage, j)

    def group(jobs):
        def source(i):
            part, j = jobs[i // i_part]
            row = (me ^ code(part, j)) * i_block + part * i_part
            if i_part % 8 == 0:
                return row // 8 + (i % i_part) // 8, i % 8
            return row // 8, (part * i_part) % 8 + i % i_part

        def pairs(state, interior, x, i):
            _, turned_ref, first_ref, grad_ref, _ = state
            pieces = []
            for lane in range(0, lanes, 128):
                cut = slice(lane, lane + 128)
                wide, narrow = [], []
                for a in range(comps):
                    lines = []
                    for j in range(joint):
                        lead, sub = source(i + j)
                        line = turned_ref[interior[x], a, lead, sub:sub + 1, cut]
                        lines.append(jnp.broadcast_to(line, (own, 128)))
                    wide.append(jnp.concatenate(lines, 0))
                    half = wide[-1][:16].astype(BF16)
                    narrow.append(jnp.concatenate([half] * (tile // 16), 0))
                row = []
                for b in range(comps):
                    phis = wide if b == 0 else narrow
                    slope = [first_ref[x, a, :, cut] if b == 0 else grad_ref[x, b - 1, a, :, cut]
                             for a in range(comps)]
                    pair = phis[0] * slope[0]
                    for a in range(1, comps):
                        pair = pair + phis[a] * slope[a]
                    row.append(pair.astype(BF16))
                pieces.append(row)
            return [pieces[l][b] for b in range(comps) for l in range(lanes // 128)]

        total = None
        for state, interior in zip(states, rows_of):
            k_rows = K_ROWS if len(interior) % K_ROWS == 0 else 6
            for first in range(0, len(interior), k_rows):
                count = min(k_rows, len(interior) - first)
                left = jnp.concatenate([
                    jnp.concatenate(
                        [p for x in range(first, first + count) for p in pairs(state, interior, x, i)], 1
                    )
                    for i in range(0, len(jobs) * i_part, joint)
                ], 0)
                right = jnp.concatenate(
                    [state[0][row].reshape(depth, width) for row in interior[first:first + count]], 0
                )
                term = jnp.dot(left, right, preferred_element_type=F32)
                total = term if total is None else total + term
        return total.reshape(len(jobs), i_part * own, width)

    jobs = [(part, j) for part, count, _, _ in parts for j in range(count)]
    at_once = group_rows(lanes) // i_part

    def put(n, low, value):
        if prior:
            value = value + prior_refs[n][pl.ds(low, value.shape[0])]
        out_refs[n][pl.ds(low, value.shape[0]), :i_part * own] = value.astype(out_refs[n].dtype)

    if len(jobs) <= at_once:
        value, at = group(jobs), 0
        for n, (_, count, _, _) in enumerate(parts):
            put(n, 0, value[at:at + count])
            at += count
    else:
        for n, (part, count, _, _) in enumerate(parts):
            size = min(at_once, count)

            def one(step, carry, n=n, part=part, size=size):
                low = step * size
                put(n, low, group([(part, low + j) for j in range(size)]))
                return carry

            lax.fori_loop(0, count // size, one, 0)
    for (part, count, _, _), out_ref in zip(parts, out_refs):
        if part == 0 and viscous:
            for j in range(count):
                dest = me ^ code(part, j)
                block = pl.ds(pl.multiple_of(dest * i_block, i_block), i_block)
                rows = sum(ref[block, :] for ref in visc_refs)
                rows = jnp.concatenate([rows, jnp.zeros((i_block, width - own), F32)], 1)
                fill = out_ref.shape[1] - i_part * own - i_block
                if fill:
                    rows = jnp.concatenate([rows, jnp.zeros((fill, width), F32)], 0)
                out_ref[j, i_part * own:] = rows.astype(out_ref.dtype)


def prepare(plan, masks, cells_z, idx, sources, extra, own):
    operands = list(sources) + list(extra)
    copies, interior = plan
    rows = max(at + stop - start for _, start, stop, at in copies)
    count = sum(stop - start for start, stop in interior)
    _, comps, part, width = sources[0].shape
    lanes = part * len(masks)
    tile = max(own, 16)
    batch = count if lanes <= 128 else max(1, 2048 // lanes)
    return pl.pallas_call(
        functools.partial(prepare_kernel, plan, masks, cells_z, tile // own),
        out_shape=(
            jax.ShapeDtypeStruct((rows, comps, lanes, width), BF16),
            jax.ShapeDtypeStruct((rows, comps, width // 8, 8, lanes), F32),
            jax.ShapeDtypeStruct((count, comps, tile, lanes), F32),
            jax.ShapeDtypeStruct((count, comps - 1, comps, tile, lanes), BF16),
            jax.ShapeDtypeStruct((width, own), F32),
        ),
        in_specs=[SMEM] + [VMEM] * len(operands),
        out_specs=(VMEM,) * 5,
        scratch_shapes=[
            pltpu.VMEM((width, batch * comps * comps * lanes), BF16),
            pltpu.VMEM((own, batch * comps * comps * lanes), BF16),
        ],
        compiler_params=pltpu.CompilerParams(vmem_limit_bytes=vmem_limit(lanes)),
        name="prepare",
    )(idx, *operands)


def project(plans, stage, parts, idx, states, own, peers, dtype, prior=(), viscous=True, earlier=()):
    _, comps, lanes, width = states[0][0].shape
    i_block = width // peers
    i_part = i_block // PARTS
    count = 1 if stage is None else peers >> (stage + 1)
    sizes = [i_part * own + (max(16, i_block) if part == 0 and viscous else 0) for part in parts]
    depth = sum(state[3].shape[0] for state in states) * comps * lanes
    flops = 2 * len(parts) * count * i_part * own * depth * width
    layout = [(part, count, i_block, i_part) for part in parts]
    operands = [array for state in states for array in state] + list(prior)
    operands += [state[4] for state in earlier]
    return pl.pallas_call(
        functools.partial(main_kernel, plans, own, stage, layout, bool(prior), viscous, len(earlier)),
        out_shape=[jax.ShapeDtypeStruct((count, rows, width), dtype) for rows in sizes],
        in_specs=[SMEM] + [VMEM] * len(operands),
        out_specs=[VMEM] * len(parts),
        compiler_params=pltpu.CompilerParams(vmem_limit_bytes=vmem_limit(lanes)),
        cost_estimate=pl.CostEstimate(flops=4 * flops, bytes_accessed=2**20, transcendentals=0),
        name="project",
    )(idx, *operands)


def arrived(results, part, code):
    found = []
    for stage, blocks in enumerate(results):
        for j in range(blocks.shape[0]):
            if code_of(part, stage, j) ^ (1 << bit_of(part, stage)) == code:
                found.append(blocks[j].astype(F32))
    return sum(found)


def finish_kernel(scales, terms, *refs):
    convective_ref, viscous_ref = refs[-2:]
    i_block, own, width = convective_ref.shape
    i_part = i_block // len(terms)
    for part, found in enumerate(terms):
        total = sum(refs[n][0, start:stop].astype(F32) for n, start, stop in found)
        rows = total[:i_part * own] * scales[0]
        convective_ref[part * i_part:(part + 1) * i_part] = rows.reshape(i_part, own, width)
        if part == 0:
            viscous_ref[...] = total[i_part * own:i_part * own + i_block, :own] * scales[1]


def body(modes):
    cells_x, cells_y, cells_z, comps, width = modes.shape
    peers_x, peers_y = lax.axis_size("gx"), lax.axis_size("gy")
    total_points = cells_x * cells_y * cells_z * peers_x * peers_y
    own = width // peers_y
    i_block = width // peers_x
    i_part = i_block // PARTS
    idx = jnp.stack([lax.axis_index("gy"), lax.axis_index("gx")]).astype(jnp.int32)
    block = modes.transpose(0, 3, 1, 2, 4).reshape(cells_x, comps, cells_y * cells_z, width)
    up = [(i, (i + 1) % peers_x) for i in range(peers_x)]
    down = [(j, i) for i, j in up]
    quarter = cells_x // 4
    middle = block[quarter - 2:cells_x - quarter + 2]
    before = lax.ppermute(block[-2:], "gx", up)
    after = lax.ppermute(block[:2], "gx", down)
    pieces, masks, (before, after) = gathered(middle, "gy", (before, after))
    length = middle.shape[0]
    plans = (
        (((0, 0, length, 0),), ((2, length - 2),)),
        (
            ((1, 0, quarter, 0), (0, 0, 4, quarter), (0, length - 4, length, quarter + 4),
             (1, quarter, 2 * quarter, quarter + 8)),
            ((2, quarter + 2), (quarter + 6, 2 * quarter + 6)),
        ),
    )
    stages = peers_x.bit_length() - 1
    both = tuple(range(PARTS))
    results = [[], []]
    states = [prepare(plans[0], masks, cells_z, idx, pieces, (), own)]
    begun = project(plans[:1], 0, both, idx, states, own, peers_x, F32, viscous=False)
    rim = gathered_stack(
        jnp.concatenate([before, block[:quarter - 2], block[cells_x - quarter + 2:], after], 0),
        "gy", begun[0],
    )
    states.append(prepare(plans[1], masks, cells_z, idx, pieces, (rim, states[0][1]), own))
    sends = project(plans[1:], 0, both, idx, states[1:], own, peers_x, BF16, prior=begun, earlier=states[:1])
    for part in both:
        results[part].append(swap(sends[part], "gx", 1 << bit_of(part, 0)))
    idx, sends = lax.optimization_barrier((idx, sends))
    for stage in range(1, stages):
        kept = project(plans, stage, both, idx, states, own, peers_x, F32)
        sums = [
            jnp.stack([kept[part][j] + arrived(results[part], part, code_of(part, stage, j))
                       for j in range(kept[part].shape[0])]).astype(BF16)
            for part in both
        ]
        if bit_of(0, stage) == bit_of(1, stage):
            rows = sums[0].shape[1]
            joined = swap(jnp.concatenate(sums, 1), "gx", 1 << stage)
            got = [joined[:, :rows], joined[:, rows:]]
        else:
            got = [swap(sums[part], "gx", 1 << bit_of(part, stage)) for part in both]
        for part in both:
            results[part].append(got[part])
        idx, sums = lax.optimization_barrier((idx, sums))
    kept = project(plans, None, both, idx, states, own, peers_x, F32)
    scales = (-1.0 / math.sqrt(total_points), -1.0 / total_points)
    blocks, terms = [], []
    for part in both:
        rows = kept[part].shape[1]
        blocks += [kept[part]] + results[part][:-1]
        terms.append([(n, 0, rows) for n in range(len(blocks) - stages, len(blocks))])
        terms[part].append((stages * len(both), sum(k.shape[1] for k in kept[:part]), sum(k.shape[1] for k in kept[:part + 1])))
    convective, viscous = pl.pallas_call(
        functools.partial(finish_kernel, scales, terms),
        out_shape=(
            jax.ShapeDtypeStruct((i_block, own, width), F32),
            jax.ShapeDtypeStruct((i_block, own), F32),
        ),
        in_specs=[VMEM] * (len(blocks) + 1),
        out_specs=(VMEM,) * 2,
        compiler_params=pltpu.CompilerParams(vmem_limit_bytes=4 * 2**20),
        name="finish",
    )(*blocks, joined)
    return (convective, viscous)


def solution(mesh):
    in_specs = (P("gx", "gy", None, None, None),)
    out_specs = (P("gx", "gy", None), P("gx", "gy"))
    return jax.shard_map(body, mesh=mesh, in_specs=in_specs, out_specs=out_specs, check_vma=False)
```

```python
import functools
import math

import jax
import jax.numpy as jnp
from jax import lax
from jax.experimental import pallas as pl
from jax.experimental.pallas import tpu as pltpu
from jax.sharding import PartitionSpec as P

BF16, F32 = jnp.bfloat16, jnp.float32
VMEM = pl.BlockSpec(memory_space=pltpu.VMEM)
SMEM = pl.BlockSpec(memory_space=pltpu.SMEM)
PARTS = 2
K_ROWS = 4


def group_rows(lanes):
    return 32 if lanes <= 128 else 8


def vmem_limit(lanes):
    return min(52, 16 * -(-lanes // 128)) * 2**20


def swap(x, axis, mask):
    return lax.ppermute(x, axis, [(i, i ^ mask) for i in range(lax.axis_size(axis))])


def gathered(x, axis, beside):
    pieces, masks, mask = [x], [0], lax.axis_size(axis) // 2
    first = True
    while mask:
        got = [swap(piece, axis, mask) for piece in pieces]
        if first:
            got, beside = lax.optimization_barrier((got, beside))
            first = False
        pieces += got
        masks += [m ^ mask for m in masks]
        mask //= 2
    return pieces, masks, beside


def gathered_stack(x, axis, behind):
    stack, mask = x[None], lax.axis_size(axis) // 2
    while mask:
        got = swap(stack, axis, mask)
        if behind is not None:
            stack, got, behind = *lax.optimization_barrier((stack, got, behind))[:2], None
        stack = jnp.concatenate([stack, got], 0)
        mask //= 2
    return stack


def y_and_z_weights(lanes, cells_z):
    q = lax.broadcasted_iota(jnp.int32, (lanes, lanes), 0)
    p = lax.broadcasted_iota(jnp.int32, (lanes, lanes), 1)
    apart = q - p
    around = jnp.where(apart < 0, apart + lanes, apart)
    same = lax.div(q, cells_z) == lax.div(p, cells_z)
    weights_y = jnp.zeros((lanes, lanes), F32)
    weights_z = jnp.zeros((lanes, lanes), F32)
    for step, weight in ((1, 8.0), (-1, -8.0), (2, -1.0), (-2, 1.0)):
        weights_y = weights_y + jnp.where(around == (step * cells_z) % lanes, weight, 0.0)
        weights_z = weights_z + jnp.where(same & (apart == step), weight, 0.0)
    return jnp.concatenate([weights_y, weights_z], 1).astype(BF16)


def prepare_kernel(plan, masks, cells_z, repeat, idx_ref, *refs):
    copies, interior = plan
    pieces = len(masks)
    extra = 2 if any(source for source, *_ in copies) else 0
    sources = [refs[:pieces]]
    if extra:
        sources.append([refs[pieces].at[q] for q in range(pieces)])
    full_ref, turned_ref, first_ref, grad_ref, visc_ref, every_ref, mine_ref = refs[pieces + extra:]
    rows, comps, lanes, width = full_ref.shape
    part = lanes // pieces
    me = idx_ref[0]
    own = width // pieces
    for q, mask in enumerate(masks):
        slot = pl.multiple_of((me ^ mask) * part, part)
        for source, start, stop, at in copies:
            full_ref[at:at + stop - start, :, pl.ds(slot, part), :] = sources[source][q][start:stop]

    def turn(row, carry):
        for comp in range(comps):
            flat = full_ref[row, comp].astype(F32).T
            turned_ref[row, comp] = flat.reshape(width // 8, 8, lanes)
        return carry

    for source, start, stop, at in copies:
        count = stop - start
        if extra and source == 0:
            turned_ref[at:at + count] = refs[pieces + 1][start:stop]
        else:
            lax.fori_loop(at, at + count, turn, 0, unroll=count if count % 4 else 4)
    weights = y_and_z_weights(lanes, cells_z)

    def derivatives(line):
        along_x = (8.0 * (line(1) - line(-1)) - (line(2) - line(-2))) * (1.0 / 12.0)
        others = jnp.dot(line(0).astype(BF16), weights, preferred_element_type=F32) * (1.0 / 12.0)
        return [value.astype(BF16) for value in (along_x, others[:, :lanes], others[:, lanes:])]

    def slopes(at, slot, row):
        mine, every = [], []
        for comp in range(comps):
            def all_rows(step):
                return turned_ref[row + step, comp].reshape(width, lanes)

            def own_rows(step):
                return turned_ref[row + step, comp, pl.ds(me * (own // 8), own // 8)].reshape(own, lanes)

            every += derivatives(all_rows)
            for b, block in enumerate(derivatives(own_rows)):
                mine.append(block)
                tiled = jnp.concatenate([block] * repeat, 0)
                if b == 0:
                    first_ref[at, comp] = tiled.astype(F32)
                else:
                    grad_ref[at, b - 1, comp] = tiled
        column = slot * (comps * comps * lanes)
        if not isinstance(slot, int):
            column = pl.multiple_of(column, lanes)
        column = pl.ds(column, comps * comps * lanes)
        every_ref[:, column] = jnp.concatenate(every, 1)
        mine_ref[:, column] = jnp.concatenate(mine, 1)

    batch = mine_ref.shape[1] // (comps * comps * lanes)
    if lanes <= 128:
        steps = [[row for start, stop in interior for row in range(start, stop)]]
    else:
        steps = [list(range(row, min(row + batch, stop))) for start, stop in interior for row in range(start, stop, batch)]
    at = 0
    for rows_now in steps:
        if lanes <= 128:
            for slot, row in enumerate(rows_now):
                slopes(at + slot, slot, row)
        else:
            def one(step, carry, start=rows_now[0], at=at):
                slopes(at + step, step, start + step)
                return carry

            lax.fori_loop(0, len(rows_now), one, 0)
        used = len(rows_now) * comps * comps * lanes
        term = lax.dot_general(
            every_ref[:, :used], mine_ref[:, :used], (((1,), (1,)), ((), ())), preferred_element_type=F32
        )
        visc_ref[...] = term if at == 0 else visc_ref[...] + term
        at += len(rows_now)


def code_of(part, stage, j):
    if part == 0 or stage >= 2:
        return (2 * j + 1) << stage
    if stage == 0:
        return (j & 1) | 2 | ((j >> 1) << 2)
    return 1 | (j << 2)


def bit_of(part, stage):
    return 1 - stage if part == 1 and stage < 2 else stage


def main_kernel(plans, own, stage, parts, prior, viscous, earlier, idx_ref, *refs):
    states = [refs[5 * n:5 * n + 5] for n in range(len(plans))]
    prior_refs = refs[5 * len(plans):5 * len(plans) + (len(parts) if prior else 0)]
    out_refs = refs[len(refs) - len(parts):]
    visc_refs = [state[4] for state in states] + list(refs[len(refs) - len(parts) - earlier:len(refs) - len(parts)])
    rows_of = [[r for start, stop in plan[1] for r in range(start, stop)] for plan in plans]
    _, comps, lanes, width = states[0][0].shape
    i_block, i_part = parts[0][2], parts[0][3]
    tile = states[0][3].shape[3]
    joint = tile // own
    me = idx_ref[1]
    depth = comps * lanes

    def code(part, j):
        return 0 if stage is None else code_of(part, stage, j)

    def group(jobs):
        def source(i):
            part, j = jobs[i // i_part]
            row = (me ^ code(part, j)) * i_block + part * i_part
            if i_part % 8 == 0:
                return row // 8 + (i % i_part) // 8, i % 8
            return row // 8, (part * i_part) % 8 + i % i_part

        def pairs(state, interior, x, i):
            _, turned_ref, first_ref, grad_ref, _ = state
            pieces = []
            for lane in range(0, lanes, 128):
                cut = slice(lane, lane + 128)
                wide, narrow = [], []
                for a in range(comps):
                    lines = []
                    for j in range(joint):
                        lead, sub = source(i + j)
                        line = turned_ref[interior[x], a, lead, sub:sub + 1, cut]
                        lines.append(jnp.broadcast_to(line, (own, 128)))
                    wide.append(jnp.concatenate(lines, 0))
                    half = wide[-1][:16].astype(BF16)
                    narrow.append(jnp.concatenate([half] * (tile // 16), 0))
                row = []
                for b in range(comps):
                    phis = wide if b == 0 else narrow
                    slope = [first_ref[x, a, :, cut] if b == 0 else grad_ref[x, b - 1, a, :, cut]
                             for a in range(comps)]
                    pair = phis[0] * slope[0]
                    for a in range(1, comps):
                        pair = pair + phis[a] * slope[a]
                    row.append(pair.astype(BF16))
                pieces.append(row)
            return [pieces[l][b] for b in range(comps) for l in range(lanes // 128)]

        total = None
        for state, interior in zip(states, rows_of):
            k_rows = K_ROWS if len(interior) % K_ROWS == 0 else 6
            for first in range(0, len(interior), k_rows):
                count = min(k_rows, len(interior) - first)
                left = jnp.concatenate([
                    jnp.concatenate(
                        [p for x in range(first, first + count) for p in pairs(state, interior, x, i)], 1
                    )
                    for i in range(0, len(jobs) * i_part, joint)
                ], 0)
                right = jnp.concatenate(
                    [state[0][row].reshape(depth, width) for row in interior[first:first + count]], 0
                )
                term = jnp.dot(left, right, preferred_element_type=F32)
                total = term if total is None else total + term
        return total.reshape(len(jobs), i_part * own, width)

    jobs = [(part, j) for part, count, _, _ in parts for j in range(count)]
    at_once = group_rows(lanes) // i_part

    def put(n, low, value):
        if prior:
            value = value + prior_refs[n][pl.ds(low, value.shape[0])]
        out_refs[n][pl.ds(low, value.shape[0]), :i_part * own] = value.astype(out_refs[n].dtype)

    if len(jobs) <= at_once:
        value, at = group(jobs), 0
        for n, (_, count, _, _) in enumerate(parts):
            put(n, 0, value[at:at + count])
            at += count
    else:
        for n, (part, count, _, _) in enumerate(parts):
            size = min(at_once, count)

            def one(step, carry, n=n, part=part, size=size):
                low = step * size
                put(n, low, group([(part, low + j) for j in range(size)]))
                return carry

            lax.fori_loop(0, count // size, one, 0)
    for (part, count, _, _), out_ref in zip(parts, out_refs):
        if part == 0 and viscous:
            for j in range(count):
                dest = me ^ code(part, j)
                block = pl.ds(pl.multiple_of(dest * i_block, i_block), i_block)
                rows = sum(ref[block, :] for ref in visc_refs)
                rows = jnp.concatenate([rows, jnp.zeros((i_block, width - own), F32)], 1)
                fill = out_ref.shape[1] - i_part * own - i_block
                if fill:
                    rows = jnp.concatenate([rows, jnp.zeros((fill, width), F32)], 0)
                out_ref[j, i_part * own:] = rows.astype(out_ref.dtype)


def prepare(plan, masks, cells_z, idx, sources, extra, own):
    operands = list(sources) + list(extra)
    copies, interior = plan
    rows = max(at + stop - start for _, start, stop, at in copies)
    count = sum(stop - start for start, stop in interior)
    _, comps, part, width = sources[0].shape
    lanes = part * len(masks)
    tile = max(own, 16)
    batch = count if lanes <= 128 else max(1, 2048 // lanes)
    return pl.pallas_call(
        functools.partial(prepare_kernel, plan, masks, cells_z, tile // own),
        out_shape=(
            jax.ShapeDtypeStruct((rows, comps, lanes, width), BF16),
            jax.ShapeDtypeStruct((rows, comps, width // 8, 8, lanes), F32),
            jax.ShapeDtypeStruct((count, comps, tile, lanes), F32),
            jax.ShapeDtypeStruct((count, comps - 1, comps, tile, lanes), BF16),
            jax.ShapeDtypeStruct((width, own), F32),
        ),
        in_specs=[SMEM] + [VMEM] * len(operands),
        out_specs=(VMEM,) * 5,
        scratch_shapes=[
            pltpu.VMEM((width, batch * comps * comps * lanes), BF16),
            pltpu.VMEM((own, batch * comps * comps * lanes), BF16),
        ],
        compiler_params=pltpu.CompilerParams(vmem_limit_bytes=vmem_limit(lanes)),
        name="prepare",
    )(idx, *operands)


def project(plans, stage, parts, idx, states, own, peers, dtype, prior=(), viscous=True, earlier=()):
    _, comps, lanes, width = states[0][0].shape
    i_block = width // peers
    i_part = i_block // PARTS
    count = 1 if stage is None else peers >> (stage + 1)
    sizes = [i_part * own + (max(16, i_block) if part == 0 and viscous else 0) for part in parts]
    depth = sum(state[3].shape[0] for state in states) * comps * lanes
    flops = 2 * len(parts) * count * i_part * own * depth * width
    layout = [(part, count, i_block, i_part) for part in parts]
    operands = [array for state in states for array in state] + list(prior)
    operands += [state[4] for state in earlier]
    return pl.pallas_call(
        functools.partial(main_kernel, plans, own, stage, layout, bool(prior), viscous, len(earlier)),
        out_shape=[jax.ShapeDtypeStruct((count, rows, width), dtype) for rows in sizes],
        in_specs=[SMEM] + [VMEM] * len(operands),
        out_specs=[VMEM] * len(parts),
        compiler_params=pltpu.CompilerParams(vmem_limit_bytes=vmem_limit(lanes)),
        cost_estimate=pl.CostEstimate(flops=4 * flops, bytes_accessed=2**20, transcendentals=0),
        name="project",
    )(idx, *operands)


def arrived(results, part, code):
    found = []
    for stage, blocks in enumerate(results):
        for j in range(blocks.shape[0]):
            if code_of(part, stage, j) ^ (1 << bit_of(part, stage)) == code:
                found.append(blocks[j].astype(F32))
    return sum(found)


def finish_kernel(scales, terms, *refs):
    convective_ref, viscous_ref = refs[-2:]
    i_block, own, width = convective_ref.shape
    i_part = i_block // len(terms)
    for part, found in enumerate(terms):
        total = sum(refs[n][0, start:stop].astype(F32) for n, start, stop in found)
        rows = total[:i_part * own] * scales[0]
        convective_ref[part * i_part:(part + 1) * i_part] = rows.reshape(i_part, own, width)
        if part == 0:
            viscous_ref[...] = total[i_part * own:i_part * own + i_block, :own] * scales[1]


def body(modes):
    cells_x, cells_y, cells_z, comps, width = modes.shape
    peers_x, peers_y = lax.axis_size("gx"), lax.axis_size("gy")
    total_points = cells_x * cells_y * cells_z * peers_x * peers_y
    own = width // peers_y
    i_block = width // peers_x
    i_part = i_block // PARTS
    idx = jnp.stack([lax.axis_index("gy"), lax.axis_index("gx")]).astype(jnp.int32)
    block = modes.transpose(0, 3, 1, 2, 4).reshape(cells_x, comps, cells_y * cells_z, width)
    up = [(i, (i + 1) % peers_x) for i in range(peers_x)]
    down = [(j, i) for i, j in up]
    quarter = cells_x // 4
    middle = block[quarter - 2:cells_x - quarter + 2]
    before = lax.ppermute(block[-2:], "gx", up)
    after = lax.ppermute(block[:2], "gx", down)
    pieces, masks, (before, after) = gathered(middle, "gy", (before, after))
    length = middle.shape[0]
    plans = (
        (((0, 0, length, 0),), ((2, length - 2),)),
        (
            ((1, 0, quarter, 0), (0, 0, 4, quarter), (0, length - 4, length, quarter + 4),
             (1, quarter, 2 * quarter, quarter + 8)),
            ((2, quarter + 2), (quarter + 6, 2 * quarter + 6)),
        ),
    )
    stages = peers_x.bit_length() - 1
    both = tuple(range(PARTS))
    results = [[], []]
    states = [prepare(plans[0], masks, cells_z, idx, pieces, (), own)]
    begun = []
    for part in both:
        begun += project(plans[:1], 0, (part,), idx, states, own, peers_x, F32, viscous=False)
    rim = gathered_stack(
        jnp.concatenate([before, block[:quarter - 2], block[cells_x - quarter + 2:], after], 0),
        "gy", begun[0],
    )
    states.append(prepare(plans[1], masks, cells_z, idx, pieces, (rim, states[0][1]), own))
    sends = project(plans[1:], 0, both, idx, states[1:], own, peers_x, BF16, prior=begun, earlier=states[:1])
    for part in both:
        results[part].append(swap(sends[part], "gx", 1 << bit_of(part, 0)))
    idx, sends = lax.optimization_barrier((idx, sends))
    for stage in range(1, stages):
        kept = project(plans, stage, both, idx, states, own, peers_x, F32)
        sums = [
            jnp.stack([kept[part][j] + arrived(results[part], part, code_of(part, stage, j))
                       for j in range(kept[part].shape[0])]).astype(BF16)
            for part in both
        ]
        if bit_of(0, stage) == bit_of(1, stage):
            rows = sums[0].shape[1]
            joined = swap(jnp.concatenate(sums, 1), "gx", 1 << stage)
            got = [joined[:, :rows], joined[:, rows:]]
        else:
            got = [swap(sums[part], "gx", 1 << bit_of(part, stage)) for part in both]
        for part in both:
            results[part].append(got[part])
        idx, sums = lax.optimization_barrier((idx, sums))
    kept = project(plans, None, both, idx, states, own, peers_x, F32)
    scales = (-1.0 / math.sqrt(total_points), -1.0 / total_points)
    blocks, terms = [], []
    for part in both:
        rows = kept[part].shape[1]
        blocks += [kept[part]] + results[part][:-1]
        terms.append([(n, 0, rows) for n in range(len(blocks) - stages, len(blocks))])
        terms[part].append((stages * len(both), sum(k.shape[1] for k in kept[:part]), sum(k.shape[1] for k in kept[:part + 1])))
    convective, viscous = pl.pallas_call(
        functools.partial(finish_kernel, scales, terms),
        out_shape=(
            jax.ShapeDtypeStruct((i_block, own, width), F32),
            jax.ShapeDtypeStruct((i_block, own), F32),
        ),
        in_specs=[VMEM] * (len(blocks) + 1),
        out_specs=(VMEM,) * 2,
        compiler_params=pltpu.CompilerParams(vmem_limit_bytes=4 * 2**20),
        name="finish",
    )(*blocks, joined)
    return (convective, viscous)


def solution(mesh):
    in_specs = (P("gx", "gy", None, None, None),)
    out_specs = (P("gx", "gy", None), P("gx", "gy"))
    return jax.shard_map(body, mesh=mesh, in_specs=in_specs, out_specs=out_specs, check_vma=False)
```
